32 devices in a mesh: groups: 2 (over x), sector: 8 (over z, y), mpo: 2 (over core).
Axes of the slice: x: 2, y: 2, z: 4, core: 2. Of those that a mesh axis runs over, the one named last changes fastest.
Arguments:
- psi: bfloat16 [128, 256, 256], P(('groups', 'sector')), parts along dimension 0, may hold values from -4 to 4
- left_env: bfloat16 [52, 64, 256, 256], P(('groups', 'mpo'), 'sector'), parts along dimension 0, may hold values from -0.375 to 0.375
- right_env: bfloat16 [52, 64, 256, 256], P(('groups', 'mpo'), 'sector'), parts along dimension 0, may hold values from -0.375 to 0.375
- term_class: int32 [52], P(('groups', 'mpo')), parts along dimension 0, may hold values from 0 to 4
- active: int32 [52, 64], P(('groups', 'mpo'), 'sector'), parts along dimension 0, may hold values 0 or 1
- dest: int32 [10, 64], P('groups', 'sector'), parts along dimension 0, may hold values from 0 to 63, as said below
- sector_rows: int32 [128], P(('groups', 'sector')), parts along dimension 0, may hold values from 64 to 256
Outputs:
- h_psi: bfloat16 [128, 256, 256], P(('groups', 'sector'), 'mpo'), parts along dimension 0
The draws below stay inside these ranges and needn't reach their ends.
There are 2 independent parts, one for each index of `groups`. The reference program is written for one: setup_inputs(seed, part) draws one part's arguments, and reference() takes and returns one part's arrays. A program takes and returns all parts, laid end to end along the dimension named above; each array names one. Nothing has to cross between parts.
Inputs may be any that keep to these rules, and one draw needn't show every extreme that they name: For each shift c, dest[c] is a permutation of the 64 sectors. Sector s = d * 8 + i goes to sector ((d + k) mod 8) * 8 + p, where k and p depend on c and i only; over all c and i, no value of k occurs more than 6 times, and some value occurs exactly 6 times.
All inputs are finite; a program needn't handle non-finite values. No bound on the sum of `active` on one device may be relied on, other than what follows from the above.
Results may differ from the reference program's by a relative error of at most 0.01.
Values may be sent and summed in bfloat16 or wider, within the bound.
No kernel may reach another device: no remote copies, remote signals or barrier semaphores. Data moves between devices by JAX's collectives and lax.ppermute only.
A program may use at most 192 MiB of HBM per device.

```python
import jax
import jax.numpy as jnp
from jax import lax

BLK = 256
W = 26
NCLS = 5
SEC_DEV = 8
SECTORS = 64
CAP = 6
N_SECTOR = 8


def draw_dest(key, part):
    key = jax.random.fold_in(key, 7)
    first, second, third = jax.random.split(key, 3)
    count = NCLS * SEC_DEV
    offset_ids = jnp.arange(N_SECTOR, dtype=jnp.int32)
    scores = jax.random.permutation(first, N_SECTOR).astype(jnp.int32)
    scores = jnp.where(offset_ids == N_SECTOR // 2, -1, scores)
    scores = jnp.where(offset_ids == N_SECTOR - 1, -2, scores)
    scores = jnp.where(offset_ids == 1 % N_SECTOR, -3, scores)
    values = jnp.argsort(scores, stable=True).astype(jnp.int32)
    pool = jnp.repeat(values, CAP)[:count]
    order = jax.random.permutation(second, count)
    offsets = pool[order].reshape(NCLS, SEC_DEV)
    locals_perm = jax.vmap(lambda kk: jax.random.permutation(kk, SEC_DEV))(jax.random.split(third, NCLS))
    devices = jnp.arange(N_SECTOR, dtype=jnp.int32)
    target_dev = (devices[None, :, None] + offsets[:, None, :]) % N_SECTOR
    target = target_dev * SEC_DEV + locals_perm[:, None, :]
    return target.reshape(NCLS, N_SECTOR * SEC_DEV).astype(jnp.int32)


def set_ends(array, rng, least, top_value):
    longest = array.shape.index(max(array.shape))
    spots = []
    for shift in (0, 1):
        where = [jax.random.randint(jax.random.fold_in(rng, axis), (), 0, length) for axis, length in enumerate(array.shape)]
        where[longest] = (where[longest] + shift) % array.shape[longest]
        spots.append(tuple(where))
    return array.at[spots[0]].set(least).at[spots[1]].set(top_value)


def level_of(stream_key, dims, pieces, low, top_value):
    def one(position, blocks):
        draws = jax.random.uniform(jax.random.fold_in(jax.random.fold_in(stream_key, 6), position), (blocks,), jnp.float32, low / len(pieces), top_value / len(pieces))
        return jnp.repeat(jnp.exp(draws), dims[position] // blocks).reshape((-1,) + (1,) * (len(dims) - position - 1))

    level = one(*pieces[0])
    for cut in pieces[1:]:
        level = level * one(*cut)
    return level


def scatter_about(stream_key, extent, scale, most, pieces=(), held_as=jnp.bfloat16):
    result = scale * jax.random.normal(stream_key, extent, jnp.float32)
    if pieces:
        result = result * level_of(stream_key, extent, pieces, -0.22, 0.18)
    return jnp.clip(result, -most, most).astype(held_as)


def setup_inputs(seed: int = 0, part: int = 0) -> dict:
    arg_keys = jax.random.split(jax.random.key(seed), 8)
    part_splits = jax.random.split(jax.random.fold_in(arg_keys[7], part), 8)
    return {
        "psi": scatter_about(part_splits[0], (SECTORS, BLK, BLK), 0.3, 4.0, ((0, 8),)),
        "left_env": scatter_about(part_splits[1], (W, SECTORS, BLK, BLK), BLK ** -0.5, 0.375, ((0, 2), (1, 8))),
        "right_env": scatter_about(part_splits[2], (W, SECTORS, BLK, BLK), BLK ** -0.5, 0.375, ((0, 2), (1, 8))),
        "term_class": set_ends(jax.random.randint(part_splits[3], (W,), 0, NCLS), jax.random.fold_in(part_splits[3], 1), 0, NCLS - 1).astype(jnp.int32),
        "active": set_ends((jax.random.randint(part_splits[4], (W, SECTORS), 0, 4) < 3).astype(jnp.int32), jax.random.fold_in(part_splits[4], 1), 0, 1),
        "dest": draw_dest(jax.random.fold_in(jax.random.fold_in(arg_keys[7], part), 71), part),
        "sector_rows": set_ends(jax.random.randint(part_splits[6], (SECTORS,), BLK // 4, BLK + 1), jax.random.fold_in(part_splits[6], 1), BLK // 4, BLK).astype(jnp.int32),
    }


def reference(psi, left_env, right_env, term_class, active, dest, sector_rows):
    line = jnp.arange(BLK, dtype=jnp.int32)
    keep = line[None, :, None] < sector_rows[:, None, None]
    masked = jnp.where(keep, psi, jnp.zeros_like(psi)).astype(jnp.bfloat16)
    picks = (term_class[None, :] == jnp.arange(NCLS, dtype=jnp.int32)[:, None]).astype(jnp.float32)
    weights = picks[:, :, None] * active[None, :, :].astype(jnp.float32)

    def one_sector(items):
        left_blocks, right_blocks, block, coef = items
        inner = jnp.einsum("wij,jk->wik", left_blocks.astype(jnp.float32), block.astype(jnp.float32),
                           precision=lax.Precision.HIGHEST).astype(jnp.bfloat16)
        terms = jnp.einsum("wij,wjk->wik", inner.astype(jnp.float32), right_blocks.astype(jnp.float32),
                           precision=lax.Precision.HIGHEST)
        return jnp.einsum("cw,wik->cik", coef, terms, precision=lax.Precision.HIGHEST)

    shifted = lax.map(one_sector, (jnp.moveaxis(left_env, 1, 0), jnp.moveaxis(right_env, 1, 0),
                                   masked, jnp.moveaxis(weights, 2, 0)))
    shifted = lax.optimization_barrier(shifted.astype(jnp.bfloat16)).astype(jnp.float32)
    total = jnp.zeros((SECTORS, BLK, BLK), jnp.float32)
    total = total.at[dest.T.reshape(-1)].add(shifted.reshape(SECTORS * NCLS, BLK, BLK))
    return jnp.where(keep, total, jnp.float32(0.0)).astype(jnp.bfloat16)
```

```python
import functools

import jax
import jax.numpy as jnp
from jax import lax
from jax.experimental import pallas as pl
from jax.experimental.pallas import tpu as pltpu
from jax.sharding import PartitionSpec as P

SMEM = pl.BlockSpec(memory_space=pltpu.SMEM)
ANY = pl.BlockSpec(memory_space=pl.ANY)
VMEM = pl.BlockSpec(memory_space=pltpu.VMEM)
DEPTH = 12
CHUNKS = 1
Y = 2


def shifts_kernel(chunk, tc, act, rows, psi, left, right, send, keep, lbuf, rbuf, acc, masked, w_of, s_of, c_of, first, sems):
    s = pl.program_id(0)
    n_w, n_s = left.shape[0], left.shape[1]
    classes = send.shape[0]
    blk = left.shape[2]
    half = blk // 2
    hr = send.shape[2]
    me = lax.axis_index("mpo")

    def copies(j):
        slot = lax.rem(j, DEPTH)
        w, sec = w_of[j], s_of[j]
        parts = [(right.at[w, sec], rbuf.at[slot])]
        if hr == half:
            parts.append((left.at[w, sec], lbuf.at[slot]))
        else:
            for h in range(2):
                parts.append((left.at[w, sec, pl.ds(h * half + chunk * hr, hr)], lbuf.at[slot, pl.ds(h * hr, hr)]))
        return [pltpu.make_async_copy(a, b, sems.at[slot, i]) for i, (a, b) in enumerate(parts)]

    def fetch(j):
        for c in copies(j):
            c.start()

    @pl.when(s == 0)
    def _():
        first[0] = 0

        def sector(sec, n):
            def term(w, n):
                on = act[w, sec]
                w_of[n] = w
                s_of[n] = sec
                c_of[n] = tc[w]

                @pl.when((on == 1) & (n < DEPTH))
                def _():
                    fetch(n)

                return n + on

            n = lax.fori_loop(0, n_w, term, n)
            odd = lax.rem(n, 2)

            @pl.when(odd == 1)
            def _():
                w_of[n] = w_of[n - 1]
                s_of[n] = sec
                c_of[n] = classes

                @pl.when(n < DEPTH)
                def _():
                    fetch(n)

            first[sec + 1] = n + odd
            return n + odd

        lax.fori_loop(0, n_s, sector, jnp.int32(0))

    total = first[n_s]
    line = lax.broadcasted_iota(jnp.int32, (blk, blk), 0)
    masked[...] = jnp.where(line < rows[s], psi[0].astype(jnp.float32), 0.0).astype(jnp.bfloat16)
    for c in range(classes):
        acc[c] = jnp.zeros(acc.shape[1:], jnp.float32)

    begin = first[s]

    def pair(t, _):
        j = begin + 2 * t
        for i in range(2):
            for c in copies(j + i):
                c.wait()
        slots = [lax.rem(j + i, DEPTH) for i in range(2)]
        inner = [
            jnp.dot(lbuf[slots[i]], masked[...], preferred_element_type=jnp.float32).astype(jnp.bfloat16)
            for i in range(2)
        ]
        terms = [jnp.dot(inner[i], rbuf[slots[i]], preferred_element_type=jnp.float32) for i in range(2)]
        for i in range(2):
            acc[c_of[j + i]] += terms[i]
        for i in range(2):

            @pl.when(j + i + DEPTH < total)
            def _():
                fetch(j + i + DEPTH)

        return 0

    lax.fori_loop(0, (first[s + 1] - begin) // 2, pair, 0)
    mine = pl.multiple_of(me * hr, hr)
    other = pl.multiple_of((1 - me) * hr, hr)
    for c in range(classes):
        keep[c, 0] = acc[c, pl.ds(mine, hr), :].astype(jnp.bfloat16)
        send[c, 0] = acc[c, pl.ds(other, hr), :].astype(jnp.bfloat16)


def shift_sums(chunk, hr, psi, left_env, right_env, term_class, active, sector_rows, classes):
    n_w, n_s, blk = left_env.shape[:3]
    out = jax.ShapeDtypeStruct((classes, n_s, hr, blk), jnp.bfloat16)
    block = pl.BlockSpec((classes, 1, hr, blk), lambda s: (0, s, 0, 0))
    most = n_s * (n_w + 1) + 1
    return pl.pallas_call(
        functools.partial(shifts_kernel, chunk),
        grid=(n_s,),
        out_shape=(out, out),
        in_specs=[SMEM, SMEM, SMEM, pl.BlockSpec((1, blk, blk), lambda s: (s, 0, 0)), ANY, ANY],
        out_specs=(block, block),
        scratch_shapes=[
            pltpu.VMEM((DEPTH, 2 * hr, blk), jnp.bfloat16),
            pltpu.VMEM((DEPTH, blk, blk), jnp.bfloat16),
            pltpu.VMEM((classes + 1, 2 * hr, blk), jnp.float32),
            pltpu.VMEM((blk, blk), jnp.bfloat16),
            pltpu.SMEM((most,), jnp.int32),
            pltpu.SMEM((most,), jnp.int32),
            pltpu.SMEM((most,), jnp.int32),
            pltpu.SMEM((n_s + 1,), jnp.int32),
            pltpu.SemaphoreType.DMA((DEPTH, 3)),
        ],
        compiler_params=pltpu.CompilerParams(vmem_limit_bytes=40 * 2**20, dimension_semantics=("arbitrary",)),
        cost_estimate=pl.CostEstimate(
            flops=4 * n_w * n_s * 2 * hr * blk * blk, bytes_accessed=2 * n_w * n_s * blk * (blk + 2 * hr), transcendentals=0
        ),
    )(term_class, active, sector_rows, psi, left_env, right_env)


def place(n, q):
    d = lax.axis_index("sector")
    z, y = d // Y, lax.rem(d, Y)
    line = n // Y
    m = jnp.where(lax.rem(z, 2) == 0, line - 1 - q, q + 1) if q < line - 1 else jnp.int32(0)
    return d, z, y, m


def scan_shift(dest, n, n_s, d, k, found):
    classes = dest.shape[0]

    def step(j, rank):
        t = dest[j // n_s, lax.rem(j, n_s)]
        hit = lax.rem(t // n_s - d + n, n) == k

        @pl.when(hit)
        def _():
            found(rank, j, lax.rem(t, n_s))

        return rank + hit.astype(jnp.int32)

    return lax.fori_loop(0, classes * n_s, step, jnp.int32(0))


def pack_kernel(n, qs, dest, keep, recv, *rest):
    outs, (a, b, sems) = rest[: len(qs)], rest[len(qs):]
    n_s = dest.shape[1]
    cap = outs[0].shape[0]
    counts = []
    for i, q in enumerate(qs):
        d, z, y, m = place(n, q)
        k = lax.rem(2 * m + 1 - 2 * y + n, n)

        def found(rank, j, p, i=i):
            pltpu.make_async_copy(keep.at[j], a.at[i, rank], sems.at[i, 0, rank]).start()
            pltpu.make_async_copy(recv.at[j], b.at[i, rank], sems.at[i, 1, rank]).start()

        counts.append(scan_shift(dest, n, n_s, d, k, found))
    for i in range(len(qs)):
        for slot in range(cap):

            @pl.when(slot < counts[i])
            def _(i=i, slot=slot):
                pltpu.make_async_copy(keep.at[0], a.at[i, slot], sems.at[i, 0, slot]).wait()
                pltpu.make_async_copy(recv.at[0], b.at[i, slot], sems.at[i, 1, slot]).wait()
                outs[i][slot] = (a[i, slot].astype(jnp.float32) + b[i, slot].astype(jnp.float32)).astype(jnp.bfloat16)


def pack(n, qs, cap, dest, keep, recv, after=()):
    hr, blk = keep.shape[1:]
    out = jax.ShapeDtypeStruct((cap, hr, blk), jnp.bfloat16)

    def body(dest, keep, recv, *rest):
        pack_kernel(n, qs, dest, keep, recv, *rest[len(after):])

    return pl.pallas_call(
        body,
        out_shape=(out,) * len(qs),
        in_specs=[SMEM, ANY, ANY] + [ANY] * len(after),
        out_specs=(VMEM,) * len(qs),
        scratch_shapes=[
            pltpu.VMEM((len(qs), cap, hr, blk), jnp.bfloat16),
            pltpu.VMEM((len(qs), cap, hr, blk), jnp.bfloat16),
            pltpu.SemaphoreType.DMA((len(qs), 2, cap)),
        ],
        compiler_params=pltpu.CompilerParams(vmem_limit_bytes=16 * 2**20),
        cost_estimate=pl.CostEstimate(flops=0, bytes_accessed=6 * len(qs) * cap * hr * blk, transcendentals=0),
    )(dest, keep, recv, *after)


def gather_kernel(n, q, chunk, dest, rows, keep, recv, crossed, *rest):
    extra, (out, a, b, total, where, sems) = rest[:-6], rest[-6:]
    n_s = dest.shape[1]
    cap = crossed.shape[0]
    hr = out.shape[1]
    d, z, y, m = place(n, q)

    def found(rank, j, p):
        where[rank] = p
        pltpu.make_async_copy(keep.at[j], a.at[rank], sems.at[0, rank]).start()
        pltpu.make_async_copy(recv.at[j], b.at[rank], sems.at[1, rank]).start()

    own = scan_shift(dest, n, n_s, d, lax.rem(2 * m, n), found)
    if extra:
        total[...] = sum(e[...].astype(jnp.float32) for e in extra)
    else:
        total[...] = jnp.zeros_like(total)

    def cross(rank, j, p):
        total[p] += crossed[rank].astype(jnp.float32)

    scan_shift(dest, n, n_s, d, lax.rem(2 * m + 2 * y - 1 + n, n), cross)
    for slot in range(cap):

        @pl.when(slot < own)
        def _(slot=slot):
            pltpu.make_async_copy(keep.at[0], a.at[slot], sems.at[0, slot]).wait()
            pltpu.make_async_copy(recv.at[0], b.at[slot], sems.at[1, slot]).wait()
            block = (a[slot].astype(jnp.float32) + b[slot].astype(jnp.float32)).astype(jnp.bfloat16)
            total[where[slot]] += block.astype(jnp.float32)

    if q == n // Y - 1:
        line = lax.broadcasted_iota(jnp.int32, total.shape[1:], 0) + (lax.axis_index("mpo") * hr * CHUNKS + chunk * hr)
        for p in range(n_s):
            out[p] = jnp.where(line < rows[p], total[p], 0.0).astype(jnp.bfloat16)
    else:
        out[...] = total[...].astype(jnp.bfloat16)


def gather(n, q, chunk, dest, rows, keep, recv, crossed, extra=()):
    hr, blk = keep.shape[1:]
    n_s = dest.shape[1]
    cap = crossed.shape[0]
    return pl.pallas_call(
        functools.partial(gather_kernel, n, q, chunk),
        out_shape=jax.ShapeDtypeStruct((n_s, hr, blk), jnp.bfloat16),
        in_specs=[SMEM, SMEM, ANY, ANY, VMEM] + [VMEM] * len(extra),
        out_specs=VMEM,
        scratch_shapes=[
            pltpu.VMEM((cap, hr, blk), jnp.bfloat16),
            pltpu.VMEM((cap, hr, blk), jnp.bfloat16),
            pltpu.VMEM((n_s, hr, blk), jnp.float32),
            pltpu.SMEM((cap,), jnp.int32),
            pltpu.SemaphoreType.DMA((2, cap)),
        ],
        compiler_params=pltpu.CompilerParams(vmem_limit_bytes=16 * 2**20),
        cost_estimate=pl.CostEstimate(flops=0, bytes_accessed=2 * (3 * cap + 2 * n_s) * hr * blk, transcendentals=0),
    )(dest, rows, keep, recv, crossed, *extra)


def body(psi, left_env, right_env, term_class, active, dest, sector_rows):
    n = lax.axis_size("sector")
    line = n // Y
    classes, n_s = dest.shape
    blk = psi.shape[1]
    half = blk // 2
    hr = half // CHUNKS
    cap = (classes * n_s + n - 1) // n + 1
    across = [(d, d ^ 1) for d in range(n)]
    near = [(z * Y + y, (z ^ 1) * Y + y) for z in range(line) for y in range(Y)]
    far = [(z * Y + y, (((z + 1) ^ 1) - 1) * Y + y) for z in range(1, line - 1) for y in range(Y)]

    outs = []
    for chunk in range(CHUNKS):
        send, keep = shift_sums(chunk, hr, psi, left_env, right_env, term_class, active, sector_rows, classes)
        send, keep = (x.reshape(classes * n_s, hr, blk) for x in (send, keep))
        recv = lax.ppermute(send, "mpo", [(0, 1), (1, 0)])
        crossed = []
        for q in range(line):
            (packed,) = pack(n, [q], cap, dest, keep, recv, crossed[-1:])
            crossed.append(lax.ppermute(packed, "sector", across))
        acc = [None] * line
        near_in, far_in = None, None
        for step in range(1, line):
            extra = () if far_in is None else (far_in,)
            acc[step - 1] = gather(n, step - 1, chunk, dest, sector_rows, keep, recv, crossed[step - 1])
            near_out = acc[step - 1]
            if far_in is not None:
                near_out = near_out + far_in
            far_out = None
            if step > 1:
                back = line - 1 - step
                if acc[back] is None:
                    acc[back] = gather(n, back, chunk, dest, sector_rows, keep, recv, crossed[back])
                far_out = acc[back] + near_in
            near_in = lax.ppermute(near_out, "sector", near)
            far_in = None if far_out is None else lax.ppermute(far_out, "sector", far)
        outs.append(gather(n, line - 1, chunk, dest, sector_rows, keep, recv, crossed[line - 1], (near_in, far_in)))
    return outs[0] if CHUNKS == 1 else jnp.concatenate(outs, axis=1)


def solution(mesh):
    placed = (
        P(("groups", "sector"), None, None),
        P(("groups", "mpo"), "sector", None, None),
        P(("groups", "mpo"), "sector", None, None),
        P(("groups", "mpo")),
        P(("groups", "mpo"), "sector"),
        P("groups", "sector"),
        P(("groups", "sector")),
    )
    return jax.shard_map(
        body,
        mesh=mesh,
        in_specs=placed,
        out_specs=P(("groups", "sector"), "mpo", None),
        check_vma=False,
    )
```

```python
import functools

import jax
import jax.numpy as jnp
from jax import lax
from jax.experimental import pallas as pl
from jax.experimental.pallas import tpu as pltpu
from jax.sharding import PartitionSpec as P

SMEM = pl.BlockSpec(memory_space=pltpu.SMEM)
VMEM = pl.BlockSpec(memory_space=pltpu.VMEM)
Y = 2
OWN, SEND, CROSS = range(3)


def split(x, by):
    if by & (by - 1) == 0:
        return lax.shift_right_logical(x, by.bit_length() - 1), x & (by - 1)
    return x // by, lax.rem(x, by)


def wrap(x, by):
    x = jnp.where(x < 0, x + by, x)
    return jnp.where(x >= by, x - by, x)


def shifts_kernel(tc, act, rows, psi, left, right, send, keep, inner, acc):
    s = pl.program_id(0)
    n_w, blk = right.shape[0], right.shape[2]
    classes, _, half = send.shape[:3]
    me = lax.axis_index("mpo")
    line = lax.broadcasted_iota(jnp.int32, (blk, blk), 0)
    masked = jnp.where(line < rows[s], psi[0].astype(jnp.float32), 0.0).astype(jnp.bfloat16)
    for c in range(classes):
        acc[c] = jnp.zeros(acc.shape[1:], jnp.float32)
    lhs = left[...].reshape(n_w * blk, blk)
    inner[...] = jnp.dot(lhs, masked, preferred_element_type=jnp.float32).astype(jnp.bfloat16)
    for w in range(n_w):
        c = jnp.where(act[w, s] == 1, tc[w], classes)
        acc[c] += jnp.dot(inner[w * blk:(w + 1) * blk], right[w, 0], preferred_element_type=jnp.float32)
    mine = pl.multiple_of(me * half, half)
    other = pl.multiple_of((1 - me) * half, half)
    for c in range(classes):
        keep[c, 0] = acc[c, pl.ds(mine, half), :].astype(jnp.bfloat16)
        send[c, 0] = acc[c, pl.ds(other, half), :].astype(jnp.bfloat16)


def shift_sums(psi, left_env, right_env, term_class, active, sector_rows, classes):
    n_w, n_s, blk = left_env.shape[:3]
    half = blk // 2
    out = jax.ShapeDtypeStruct((classes, n_s, half, blk), jnp.bfloat16)
    block = pl.BlockSpec((classes, 1, half, blk), lambda s: (0, s, 0, 0))
    env = pl.BlockSpec((n_w, 1, blk, blk), lambda s: (0, s, 0, 0))
    return pl.pallas_call(
        shifts_kernel,
        grid=(n_s,),
        out_shape=(out, out),
        in_specs=[SMEM, SMEM, SMEM, pl.BlockSpec((1, blk, blk), lambda s: (s, 0, 0)), env, env],
        out_specs=(block, block),
        scratch_shapes=[
            pltpu.VMEM((n_w * blk, blk), jnp.bfloat16),
            pltpu.VMEM((classes + 1, blk, blk), jnp.float32),
        ],
        compiler_params=pltpu.CompilerParams(vmem_limit_bytes=40 * 2**20, dimension_semantics=("arbitrary",)),
        cost_estimate=pl.CostEstimate(
            flops=4 * n_w * n_s * blk**3, bytes_accessed=4 * n_w * n_s * blk * blk, transcendentals=0
        ),
    )(term_class, active, sector_rows, psi, left_env, right_env)


def table_at(cap, q, kind):
    return (q * 3 + kind) * (1 + 2 * cap)


def table_kernel(n, cap, dest, table):
    classes, n_s = dest.shape
    line = n // Y
    d = lax.axis_index("sector")
    z, y = split(d, Y)
    even = (z & 1) == 0

    def clear(i, _):
        table[i * (1 + 2 * cap)] = 0
        return 0

    lax.fori_loop(0, 3 * line, clear, 0)

    def position(twice):
        m = wrap(lax.shift_right_arithmetic(twice, 1), line)
        return jnp.where(m == 0, line - 1, jnp.where(even, line - 1 - m, m - 1))

    def note(q, kind, j, p):
        at = table_at(cap, q, kind)
        count = table[at]
        table[at + 1 + count] = j
        table[at + 1 + cap + count] = p
        table[at] = count + 1

    for c in range(classes):

        def step(i, _, c=c):
            t, p = split(dest[c, i], n_s)
            k = wrap(t - d, n)
            j = c * n_s + i

            @pl.when((k & 1) == 0)
            def _():
                note(position(k), OWN, j, p)

            @pl.when((k & 1) == 1)
            def _():
                note(position(k - 1 + 2 * y), SEND, j, p)
                note(position(k + 1 - 2 * y), CROSS, j, p)

            return 0

        lax.fori_loop(0, n_s, step, 0)


def make_table(n, cap, dest):
    return pl.pallas_call(
        functools.partial(table_kernel, n, cap),
        out_shape=jax.ShapeDtypeStruct((3 * (n // Y) * (1 + 2 * cap),), jnp.int32),
        in_specs=[SMEM],
        out_specs=SMEM,
        cost_estimate=pl.CostEstimate(flops=4000, bytes_accessed=4000, transcendentals=0),
    )(dest)


def joined(keep, recv, j):
    return keep[j].astype(jnp.float32) + recv[j].astype(jnp.float32)


def pack_into(out, cap, q, start, table, keep, recv):
    at = table_at(cap, q, SEND)
    rows = pl.ds(start, out.shape[1])

    def step(slot, _):
        j = table[at + 1 + slot]
        out[slot] = (keep[j, rows].astype(jnp.float32) + recv[j, rows].astype(jnp.float32)).astype(jnp.bfloat16)
        return 0

    lax.fori_loop(0, table[at], step, 0)


def pack(cap, q, pieces, table, keep, recv):
    blk = keep.shape[2]

    def kernel(table, keep, recv, *outs):
        for out, (start, size) in zip(outs, pieces):
            pack_into(out, cap, q, start, table, keep, recv)

    return pl.pallas_call(
        kernel,
        out_shape=[jax.ShapeDtypeStruct((cap, size, blk), jnp.bfloat16) for _, size in pieces],
        in_specs=[SMEM, VMEM, VMEM],
        out_specs=[VMEM] * len(pieces),
        compiler_params=pltpu.CompilerParams(vmem_limit_bytes=16 * 2**20),
        cost_estimate=pl.CostEstimate(flops=0, bytes_accessed=1000, transcendentals=0),
    )(table, keep, recv)


def pack_rest(cap, line, pieces, table, keep, recv, after):
    blk = keep.shape[2]
    flat = [(q, piece) for q in range(1, line) for piece in pieces[q]]

    def kernel(table, keep, recv, after, *packed):
        for (q, (start, _)), out in zip(flat, packed):
            pack_into(out, cap, q, start, table, keep, recv)

    outs = pl.pallas_call(
        kernel,
        out_shape=[jax.ShapeDtypeStruct((cap, size, blk), jnp.bfloat16) for _, (_, size) in flat],
        in_specs=[SMEM, VMEM, VMEM, pl.BlockSpec(memory_space=pl.ANY)],
        out_specs=[VMEM] * len(flat),
        compiler_params=pltpu.CompilerParams(vmem_limit_bytes=16 * 2**20),
        cost_estimate=pl.CostEstimate(flops=0, bytes_accessed=1000, transcendentals=0),
    )(table, keep, recv, after)
    return [[x for (at, _), x in zip(flat, outs) if at == q] for q in range(1, line)]


def add_own(cap, line, n_s, table, keep, recv, firsts):
    half, blk = keep.shape[1:]

    def kernel(table, keep, recv, *refs):
        own = refs[len(firsts):]
        for q in range(line):
            own[q][...] = jnp.zeros(own[q].shape, jnp.float32)
            at = table_at(cap, q, OWN)

            def step(slot, _, q=q, at=at):
                block = joined(keep, recv, table[at + 1 + slot]).astype(jnp.bfloat16)
                own[q][table[at + 1 + cap + slot]] += block.astype(jnp.float32)
                return 0

            lax.fori_loop(0, table[at], step, 0)

    return pl.pallas_call(
        kernel,
        out_shape=[jax.ShapeDtypeStruct((n_s, half, blk), jnp.float32)] * line,
        in_specs=[SMEM, VMEM, VMEM] + [pl.BlockSpec(memory_space=pl.ANY)] * len(firsts),
        out_specs=[VMEM] * line,
        compiler_params=pltpu.CompilerParams(vmem_limit_bytes=24 * 2**20),
        cost_estimate=pl.CostEstimate(flops=0, bytes_accessed=1000, transcendentals=0),
    )(table, keep, recv, *firsts)


def gather(cap, q, piece, table, own, crossed):
    n_s, _, blk = own.shape
    start, size = piece
    at = table_at(cap, q, CROSS)

    def kernel(table, own, crossed, out, total):
        total[...] = own[:, start:start + size]

        def step(slot, _):
            total[table[at + 1 + cap + slot]] += crossed[slot].astype(jnp.float32)
            return 0

        lax.fori_loop(0, table[at], step, 0)
        out[...] = total[...].astype(jnp.bfloat16)

    return pl.pallas_call(
        kernel,
        out_shape=jax.ShapeDtypeStruct((n_s, size, blk), jnp.bfloat16),
        in_specs=[SMEM, VMEM, VMEM],
        out_specs=VMEM,
        scratch_shapes=[pltpu.VMEM((n_s, size, blk), jnp.float32)],
        compiler_params=pltpu.CompilerParams(vmem_limit_bytes=16 * 2**20),
        cost_estimate=pl.CostEstimate(flops=0, bytes_accessed=1000, transcendentals=0),
    )(table, own, crossed)


def finish(cap, q, table, rows, own, crossed, arrived):
    n_s, half, blk = own.shape
    at = table_at(cap, q, CROSS)
    spots = [start for start, _ in arrived]

    def kernel(table, rows, own, crossed, *rest):
        parts, (out, total) = rest[:-2], rest[-2:]
        total[...] = own[...]

        def step(slot, _):
            total[table[at + 1 + cap + slot]] += crossed[slot].astype(jnp.float32)
            return 0

        lax.fori_loop(0, table[at], step, 0)
        for start, part in zip(spots, parts):
            total[:, start:start + part.shape[1]] += part[...].astype(jnp.float32)
        line = lax.broadcasted_iota(jnp.int32, (half, blk), 0) + lax.axis_index("mpo") * half
        for p in range(n_s):
            out[p] = jnp.where(line < rows[p], total[p], 0.0).astype(jnp.bfloat16)

    return pl.pallas_call(
        kernel,
        out_shape=jax.ShapeDtypeStruct((n_s, half, blk), jnp.bfloat16),
        in_specs=[SMEM, SMEM, VMEM, VMEM] + [VMEM] * len(arrived),
        out_specs=VMEM,
        scratch_shapes=[pltpu.VMEM((n_s, half, blk), jnp.float32)],
        compiler_params=pltpu.CompilerParams(vmem_limit_bytes=16 * 2**20),
        cost_estimate=pl.CostEstimate(flops=0, bytes_accessed=1000, transcendentals=0),
    )(table, rows, own, crossed, *[part for _, part in arrived])


def plus(a, a_start, b, b_start, size):
    def kernel(a, b, out):
        total = a[:, a_start:a_start + size].astype(jnp.float32) + b[:, b_start:b_start + size].astype(jnp.float32)
        out[...] = total.astype(jnp.bfloat16)

    return pl.pallas_call(
        kernel,
        out_shape=jax.ShapeDtypeStruct((a.shape[0], size, a.shape[2]), jnp.bfloat16),
        in_specs=[VMEM, VMEM],
        out_specs=VMEM,
        compiler_params=pltpu.CompilerParams(vmem_limit_bytes=16 * 2**20),
        cost_estimate=pl.CostEstimate(flops=0, bytes_accessed=1000, transcendentals=0),
    )(a, b)


def sums(a_parts, b_parts, piece):
    start, size = piece

    def holder(parts):
        for first, x in parts:
            if first <= start and start + size <= first + x.shape[1]:
                return x, start - first
        return some_rows(parts, piece), 0

    return plus(*holder(a_parts), *holder(b_parts), size)


def some_rows(parts, piece):
    start, size = piece
    got = []
    for first, part in parts:
        low, high = max(first, start), min(first + part.shape[1], start + size)
        if low < high:
            got.append(part if (low, high) == (first, first + part.shape[1]) else part[:, low - first:high - first])
    return got[0] if len(got) == 1 else jnp.concatenate(got, axis=1)


def body(psi, left_env, right_env, term_class, active, dest, sector_rows):
    n = lax.axis_size("sector")
    line = n // Y
    classes, n_s = dest.shape
    blk = psi.shape[1]
    half = blk // 2
    cap = (classes * n_s + n - 1) // n + 1
    whole = [(0, half)]
    halves = [(0, half // 2), (half // 2, half // 2)]
    across = [(d, d ^ 1) for d in range(n)]
    near = [(z * Y + y, (z ^ 1) * Y + y) for z in range(line) for y in range(Y)]
    far = [(z * Y + y, (((z + 1) ^ 1) - 1) * Y + y) for z in range(1, line - 1) for y in range(Y)]

    send, keep = shift_sums(psi, left_env, right_env, term_class, active, sector_rows, classes)
    send, keep = (x.reshape(classes * n_s, half, blk) for x in (send, keep))
    recv = lax.ppermute(send, "mpo", [(0, 1), (1, 0)])
    table = make_table(n, cap, dest)
    pieces = [halves] * (line - 1) + [whole]
    firsts = pack(cap, 0, pieces[0], table, keep, recv)
    crossed = [[lax.ppermute(x, "sector", across) for x in firsts]]
    own = add_own(cap, line, n_s, table, keep, recv, firsts)
    packed = pack_rest(cap, line, pieces, table, keep, recv, crossed[0][0])
    crossed += [[lax.ppermute(x, "sector", across) for x in xs] for xs in packed]

    acc = []
    for q in range(line - 1):
        acc.append([(piece[0], gather(cap, q, piece, table, own[q], x)) for piece, x in zip(pieces[q], crossed[q])])
    near_in, far_in = None, None
    for step in range(1, line):
        near_out, far_out = [], []
        for piece in halves:
            if far_in is None:
                near_out.append((piece[0], some_rows(acc[step - 1], piece)))
            else:
                near_out.append((piece[0], sums(acc[step - 1], far_in, piece)))
        if step > 1:
            for piece in halves:
                far_out.append((piece[0], sums(acc[line - 1 - step], near_in, piece)))
        near_in = [(start, lax.ppermute(x, "sector", near)) for start, x in near_out]
        far_in = [(start, lax.ppermute(x, "sector", far)) for start, x in far_out] if far_out else None
    return finish(cap, line - 1, table, sector_rows, own[line - 1], crossed[line - 1][0], near_in + (far_in or []))


def solution(mesh):
    placed = (
        P(("groups", "sector"), None, None),
        P(("groups", "mpo"), "sector", None, None),
        P(("groups", "mpo"), "sector", None, None),
        P(("groups", "mpo")),
        P(("groups", "mpo"), "sector"),
        P("groups", "sector"),
        P(("groups", "sector")),
    )
    return jax.shard_map(
        body,
        mesh=mesh,
        in_specs=placed,
        out_specs=P(("groups", "sector"), "mpo", None),
        check_vma=False,
    )
```

```python
import functools

import jax
import jax.numpy as jnp
from jax import lax
from jax.experimental import pallas as pl
from jax.experimental.pallas import tpu as pltpu
from jax.sharding import PartitionSpec as P

SMEM = pl.BlockSpec(memory_space=pltpu.SMEM)
VMEM = pl.BlockSpec(memory_space=pltpu.VMEM)
HBM = pl.BlockSpec(memory_space=pltpu.HBM)
Y = 2
OWN, SEND, CROSS = range(3)


def split(x, by):
    if by & (by - 1) == 0:
        return lax.shift_right_logical(x, by.bit_length() - 1), x & (by - 1)
    return x // by, lax.rem(x, by)


def wrap(x, by):
    x = jnp.where(x < 0, x + by, x)
    return jnp.where(x >= by, x - by, x)


def shifts_kernel(slots, masked, left, right, send, keep, lbuf, rbuf, inner, acc, sems):
    n_w, n_s, blk = right.shape[:3]
    classes, _, half = send.shape[:3]
    depth = lbuf.shape[0]
    me = lax.axis_index("mpo")

    def copies(s):
        at = lax.rem(s, depth)
        return (
            pltpu.make_async_copy(left.at[:, s], lbuf.at[at], sems.at[0, at]),
            pltpu.make_async_copy(right.at[:, s], rbuf.at[at], sems.at[1, at]),
        )

    for s in range(min(depth, n_s)):
        for c in copies(jnp.int32(s)):
            c.start()
    mine = pl.multiple_of(me * half, half)
    other = pl.multiple_of((1 - me) * half, half)

    def sector(s, _):
        at = lax.rem(s, depth)
        here = copies(s)
        here[0].wait()
        for c in range(classes):
            acc[c] = jnp.zeros(acc.shape[1:], jnp.float32)
        lhs = lbuf[at].reshape(n_w * blk, blk)
        inner[...] = jnp.dot(lhs, masked[s], preferred_element_type=jnp.float32).astype(jnp.bfloat16)
        here[1].wait()
        for w in range(n_w):
            acc[slots[s, w]] += jnp.dot(
                inner[w * blk:(w + 1) * blk], rbuf[at, w], preferred_element_type=jnp.float32
            )

        @pl.when(s + depth < n_s)
        def _():
            for c in copies(s + depth):
                c.start()

        for c in range(classes):
            keep[c, s] = acc[c, pl.ds(mine, half), :].astype(jnp.bfloat16)
            send[c, s] = acc[c, pl.ds(other, half), :].astype(jnp.bfloat16)
        return 0

    lax.fori_loop(0, n_s, sector, 0)


def shift_sums(psi, left_env, right_env, term_class, active, sector_rows, classes):
    n_w, n_s, blk = left_env.shape[:3]
    half = blk // 2
    depth = 3
    line = jnp.arange(blk, dtype=jnp.int32)
    masked = jnp.where(line[None, :, None] < sector_rows[:, None, None], psi, jnp.zeros_like(psi))
    slots = jnp.where(active.T == 1, term_class[None, :], classes)
    out = jax.ShapeDtypeStruct((classes, n_s, half, blk), jnp.bfloat16)
    return pl.pallas_call(
        shifts_kernel,
        out_shape=(out, out),
        in_specs=[SMEM, VMEM, HBM, HBM],
        out_specs=(VMEM, VMEM),
        scratch_shapes=[
            pltpu.VMEM((depth, n_w, blk, blk), jnp.bfloat16),
            pltpu.VMEM((depth, n_w, blk, blk), jnp.bfloat16),
            pltpu.VMEM((n_w * blk, blk), jnp.bfloat16),
            pltpu.VMEM((classes + 1, blk, blk), jnp.float32),
            pltpu.SemaphoreType.DMA((2, depth)),
        ],
        compiler_params=pltpu.CompilerParams(vmem_limit_bytes=40 * 2**20),
        cost_estimate=pl.CostEstimate(
            flops=4 * n_w * n_s * blk**3, bytes_accessed=4 * n_w * n_s * blk * blk, transcendentals=0
        ),
    )(slots, masked, left_env, right_env)


def table_at(cap, q, kind):
    return (q * 3 + kind) * (1 + 2 * cap)


def table_kernel(n, cap, dest, table):
    classes, n_s = dest.shape
    line = n // Y
    d = lax.axis_index("sector")
    z, y = split(d, Y)
    even = (z & 1) == 0

    for i in range(3 * line):
        table[i * (1 + 2 * cap)] = 0
        for slot in range(cap):
            table[i * (1 + 2 * cap) + 1 + slot] = 0
            table[i * (1 + 2 * cap) + 1 + cap + slot] = n_s

    def position(twice):
        m = wrap(lax.shift_right_arithmetic(twice, 1), line)
        return jnp.where(m == 0, line - 1, jnp.where(even, line - 1 - m, m - 1))

    def note(q, kind, j, p):
        at = table_at(cap, q, kind)
        count = table[at]
        table[at + 1 + count] = j
        table[at + 1 + cap + count] = p
        table[at] = count + 1

    for c in range(classes):

        def step(i, _, c=c):
            t, p = split(dest[c, i], n_s)
            k = wrap(t - d, n)
            j = c * n_s + i

            @pl.when((k & 1) == 0)
            def _():
                note(position(k), OWN, j, p)

            @pl.when((k & 1) == 1)
            def _():
                note(position(k - 1 + 2 * y), SEND, j, p)
                note(position(k + 1 - 2 * y), CROSS, j, p)

            return 0

        lax.fori_loop(0, n_s, step, 0)


def make_table(n, cap, dest):
    return pl.pallas_call(
        functools.partial(table_kernel, n, cap),
        out_shape=jax.ShapeDtypeStruct((3 * (n // Y) * (1 + 2 * cap),), jnp.int32),
        in_specs=[SMEM],
        out_specs=SMEM,
        cost_estimate=pl.CostEstimate(flops=4000, bytes_accessed=4000, transcendentals=0),
    )(dest)


def pack_into(out, cap, q, start, table, keep, recv):
    at = table_at(cap, q, SEND)
    rows = pl.ds(start, out.shape[1])

    for slot in range(cap):
        j = table[at + 1 + slot]
        out[slot] = keep[j, rows] + recv[j, rows]


def pack(cap, q, pieces, table, keep, recv):
    blk = keep.shape[2]

    def kernel(table, keep, recv, *outs):
        for out, (start, size) in zip(outs, pieces):
            pack_into(out, cap, q, start, table, keep, recv)

    return pl.pallas_call(
        kernel,
        out_shape=[jax.ShapeDtypeStruct((cap, size, blk), jnp.bfloat16) for _, size in pieces],
        in_specs=[SMEM, VMEM, VMEM],
        out_specs=[VMEM] * len(pieces),
        compiler_params=pltpu.CompilerParams(vmem_limit_bytes=16 * 2**20),
        cost_estimate=pl.CostEstimate(flops=0, bytes_accessed=1000, transcendentals=0),
    )(table, keep, recv)


def pack_rest(cap, line, pieces, table, keep, recv, after):
    blk = keep.shape[2]
    flat = [(q, piece) for q in range(1, line) for piece in pieces[q]]

    def kernel(table, keep, recv, after, *packed):
        for (q, (start, _)), out in zip(flat, packed):
            pack_into(out, cap, q, start, table, keep, recv)

    outs = pl.pallas_call(
        kernel,
        out_shape=[jax.ShapeDtypeStruct((cap, size, blk), jnp.bfloat16) for _, (_, size) in flat],
        in_specs=[SMEM, VMEM, VMEM, pl.BlockSpec(memory_space=pl.ANY)],
        out_specs=[VMEM] * len(flat),
        compiler_params=pltpu.CompilerParams(vmem_limit_bytes=16 * 2**20),
        cost_estimate=pl.CostEstimate(flops=0, bytes_accessed=1000, transcendentals=0),
    )(table, keep, recv, after)
    return [[x for (at, _), x in zip(flat, outs) if at == q] for q in range(1, line)]


def add_own(cap, line, n_s, table, keep, recv, firsts):
    half, blk = keep.shape[1:]

    def kernel(table, keep, recv, *refs):
        own = refs[len(firsts):]
        for q in range(line):
            own[q][...] = jnp.zeros(own[q].shape, jnp.float32)
            at = table_at(cap, q, OWN)

            for slot in range(cap):
                j = table[at + 1 + slot]
                own[q][table[at + 1 + cap + slot]] += (keep[j] + recv[j]).astype(jnp.float32)

    return pl.pallas_call(
        kernel,
        out_shape=[jax.ShapeDtypeStruct((n_s + 1, half, blk), jnp.float32)] * line,
        in_specs=[SMEM, VMEM, VMEM] + [pl.BlockSpec(memory_space=pl.ANY)] * len(firsts),
        out_specs=[VMEM] * line,
        compiler_params=pltpu.CompilerParams(vmem_limit_bytes=24 * 2**20),
        cost_estimate=pl.CostEstimate(flops=0, bytes_accessed=1000, transcendentals=0),
    )(table, keep, recv, *firsts)


def gather(cap, q, piece, table, own, crossed):
    n_s, blk = own.shape[0] - 1, own.shape[2]
    start, size = piece
    at = table_at(cap, q, CROSS)

    def kernel(table, own, crossed, out, total):
        total[:n_s] = own[:n_s, start:start + size]
        for slot in range(cap):
            total[table[at + 1 + cap + slot]] += crossed[slot].astype(jnp.float32)
        out[...] = total[:n_s].astype(jnp.bfloat16)

    return pl.pallas_call(
        kernel,
        out_shape=jax.ShapeDtypeStruct((n_s, size, blk), jnp.bfloat16),
        in_specs=[SMEM, VMEM, VMEM],
        out_specs=VMEM,
        scratch_shapes=[pltpu.VMEM((n_s + 1, size, blk), jnp.float32)],
        compiler_params=pltpu.CompilerParams(vmem_limit_bytes=16 * 2**20),
        cost_estimate=pl.CostEstimate(flops=0, bytes_accessed=1000, transcendentals=0),
    )(table, own, crossed)


def finish(cap, q, table, rows, own, crossed, arrived):
    n_s, half, blk = own.shape[0] - 1, own.shape[1], own.shape[2]
    at = table_at(cap, q, CROSS)
    spots = [start for start, _ in arrived]

    def kernel(table, rows, own, crossed, *rest):
        parts, (out, total) = rest[:-2], rest[-2:]
        total[:n_s] = own[:n_s]
        for slot in range(cap):
            total[table[at + 1 + cap + slot]] += crossed[slot].astype(jnp.float32)
        line = lax.broadcasted_iota(jnp.int32, (half, blk), 0) + lax.axis_index("mpo") * half
        for start, part in zip(spots, parts):
            total[:n_s, start:start + part.shape[1]] += part[...].astype(jnp.float32)
        for p in range(n_s):
            out[p] = jnp.where(line < rows[p], total[p], 0.0).astype(jnp.bfloat16)

    return pl.pallas_call(
        kernel,
        out_shape=jax.ShapeDtypeStruct((n_s, half, blk), jnp.bfloat16),
        in_specs=[SMEM, SMEM, VMEM, VMEM] + [VMEM] * len(arrived),
        out_specs=VMEM,
        scratch_shapes=[pltpu.VMEM((n_s + 1, half, blk), jnp.float32)],
        compiler_params=pltpu.CompilerParams(vmem_limit_bytes=16 * 2**20),
        cost_estimate=pl.CostEstimate(flops=0, bytes_accessed=1000, transcendentals=0),
    )(table, rows, own, crossed, *[part for _, part in arrived])


def plus(a, a_start, b, b_start, size):
    def kernel(a, b, out):
        total = a[:, a_start:a_start + size].astype(jnp.float32) + b[:, b_start:b_start + size].astype(jnp.float32)
        out[...] = total.astype(jnp.bfloat16)

    return pl.pallas_call(
        kernel,
        out_shape=jax.ShapeDtypeStruct((a.shape[0], size, a.shape[2]), jnp.bfloat16),
        in_specs=[VMEM, VMEM],
        out_specs=VMEM,
        compiler_params=pltpu.CompilerParams(vmem_limit_bytes=16 * 2**20),
        cost_estimate=pl.CostEstimate(flops=0, bytes_accessed=1000, transcendentals=0),
    )(a, b)


def sums(a_parts, b_parts, piece):
    start, size = piece

    def holder(parts):
        for first, x in parts:
            if first <= start and start + size <= first + x.shape[1]:
                return x, start - first
        return some_rows(parts, piece), 0

    return plus(*holder(a_parts), *holder(b_parts), size)


def some_rows(parts, piece):
    start, size = piece
    got = []
    for first, part in parts:
        low, high = max(first, start), min(first + part.shape[1], start + size)
        if low < high:
            got.append(part if (low, high) == (first, first + part.shape[1]) else part[:, low - first:high - first])
    return got[0] if len(got) == 1 else jnp.concatenate(got, axis=1)


def body(psi, left_env, right_env, term_class, active, dest, sector_rows):
    n = lax.axis_size("sector")
    line = n // Y
    classes, n_s = dest.shape
    blk = psi.shape[1]
    half = blk // 2
    cap = (classes * n_s + n - 1) // n + 1
    whole = [(0, half)]
    halves = [(0, half // 2), (half // 2, half // 2)]
    across = [(d, d ^ 1) for d in range(n)]
    near = [(z * Y + y, (z ^ 1) * Y + y) for z in range(line) for y in range(Y)]
    far = [(z * Y + y, (((z + 1) ^ 1) - 1) * Y + y) for z in range(1, line - 1) for y in range(Y)]

    send, keep = shift_sums(psi, left_env, right_env, term_class, active, sector_rows, classes)
    send, keep = (x.reshape(classes * n_s, half, blk) for x in (send, keep))
    recv = lax.ppermute(send, "mpo", [(0, 1), (1, 0)])
    table = make_table(n, cap, dest)
    pieces = [halves] * (line - 1) + [whole]
    firsts = pack(cap, 0, pieces[0], table, keep, recv)
    crossed = [[lax.ppermute(x, "sector", across) for x in firsts]]
    own = add_own(cap, line, n_s, table, keep, recv, firsts)
    packed = pack_rest(cap, line, pieces, table, keep, recv, firsts[0])
    crossed += [[lax.ppermute(x, "sector", across) for x in xs] for xs in packed]

    acc = []
    for q in range(line - 1):
        acc.append([(piece[0], gather(cap, q, piece, table, own[q], x)) for piece, x in zip(pieces[q], crossed[q])])
    near_in, far_in = None, None
    for step in range(1, line):
        near_out, far_out = [], []
        for piece in halves:
            if far_in is None:
                near_out.append((piece[0], some_rows(acc[step - 1], piece)))
            else:
                near_out.append((piece[0], sums(acc[step - 1], far_in, piece)))
        if step > 1:
            for piece in halves:
                far_out.append((piece[0], sums(acc[line - 1 - step], near_in, piece)))
        near_in = [(start, lax.ppermute(x, "sector", near)) for start, x in near_out]
        far_in = [(start, lax.ppermute(x, "sector", far)) for start, x in far_out] if far_out else None
    return finish(cap, line - 1, table, sector_rows, own[line - 1], crossed[line - 1][0], near_in + (far_in or []))


def solution(mesh):
    placed = (
        P(("groups", "sector"), None, None),
        P(("groups", "mpo"), "sector", None, None),
        P(("groups", "mpo"), "sector", None, None),
        P(("groups", "mpo")),
        P(("groups", "mpo"), "sector"),
        P("groups", "sector"),
        P(("groups", "sector")),
    )
    return jax.shard_map(
        body,
        mesh=mesh,
        in_specs=placed,
        out_specs=P(("groups", "sector"), "mpo", None),
        check_vma=False,
    )
```

```python
import functools

import jax
import jax.numpy as jnp
from jax import lax
from jax.experimental import pallas as pl
from jax.experimental.pallas import tpu as pltpu
from jax.sharding import PartitionSpec as P

SMEM = pl.BlockSpec(memory_space=pltpu.SMEM)
VMEM = pl.BlockSpec(memory_space=pltpu.VMEM)
HBM = pl.BlockSpec(memory_space=pltpu.HBM)
Y = 2
OWN, SEND, CROSS = range(3)


def split(x, by):
    if by & (by - 1) == 0:
        return lax.shift_right_logical(x, by.bit_length() - 1), x & (by - 1)
    return x // by, lax.rem(x, by)


def wrap(x, by):
    x = jnp.where(x < 0, x + by, x)
    return jnp.where(x >= by, x - by, x)


def shifts_kernel(slots, masked, left, right, *refs):
    pieces = (len(refs) - 5) // 2
    send, keep = refs[:pieces], refs[pieces:2 * pieces]
    lbuf, rbuf, inner, acc, sems = refs[2 * pieces:]
    n_w, n_s, blk = right.shape[:3]
    classes, _, size = send[0].shape[:3]
    depth = lbuf.shape[0]
    me = lax.axis_index("mpo")

    def copies(s):
        at = lax.rem(s, depth)
        return (
            pltpu.make_async_copy(left.at[:, s], lbuf.at[at], sems.at[0, at]),
            pltpu.make_async_copy(right.at[:, s], rbuf.at[at], sems.at[1, at]),
        )

    for s in range(min(depth, n_s)):
        for c in copies(jnp.int32(s)):
            c.start()

    def sector(s, _):
        at = lax.rem(s, depth)
        for c in copies(s):
            c.wait()
        for c in range(classes):
            acc[c] = jnp.zeros(acc.shape[1:], jnp.float32)
        for w in range(n_w):
            inner[w * blk:(w + 1) * blk] = jnp.dot(
                lbuf[at, w], masked[s], preferred_element_type=jnp.float32
            ).astype(jnp.bfloat16)
        for w in range(n_w):
            acc[slots[s, w]] += jnp.dot(
                inner[w * blk:(w + 1) * blk], rbuf[at, w], preferred_element_type=jnp.float32
            )

        @pl.when(s + depth < n_s)
        def _():
            for c in copies(s + depth):
                c.start()

        for piece in range(pieces):
            mine = pl.multiple_of(me * (blk // 2) + piece * size, size)
            other = pl.multiple_of((1 - me) * (blk // 2) + piece * size, size)
            for c in range(classes):
                keep[piece][c, s] = acc[c, pl.ds(mine, size), :].astype(jnp.bfloat16)
                send[piece][c, s] = acc[c, pl.ds(other, size), :].astype(jnp.bfloat16)
        return 0

    lax.fori_loop(0, n_s, sector, 0)


def shift_sums(psi, left_env, right_env, term_class, active, sector_rows, classes, pieces):
    n_w, n_s, blk = left_env.shape[:3]
    size = blk // 2 // pieces
    depth = 3
    line = jnp.arange(blk, dtype=jnp.int32)
    masked = jnp.where(line[None, :, None] < sector_rows[:, None, None], psi, jnp.zeros_like(psi))
    slots = jnp.where(active.T == 1, term_class[None, :], classes)
    outs = pl.pallas_call(
        shifts_kernel,
        out_shape=[jax.ShapeDtypeStruct((classes, n_s, size, blk), jnp.bfloat16)] * (2 * pieces),
        in_specs=[SMEM, VMEM, HBM, HBM],
        out_specs=[VMEM] * (2 * pieces),
        scratch_shapes=[
            pltpu.VMEM((depth, n_w, blk, blk), jnp.bfloat16),
            pltpu.VMEM((depth, n_w, blk, blk), jnp.bfloat16),
            pltpu.VMEM((n_w * blk, blk), jnp.bfloat16),
            pltpu.VMEM((classes + 1, blk, blk), jnp.float32),
            pltpu.SemaphoreType.DMA((2, depth)),
        ],
        compiler_params=pltpu.CompilerParams(vmem_limit_bytes=40 * 2**20),
        cost_estimate=pl.CostEstimate(
            flops=4 * n_w * n_s * blk**3, bytes_accessed=4 * n_w * n_s * blk * blk, transcendentals=0
        ),
    )(slots, masked, left_env, right_env)
    outs = [x.reshape(classes * n_s, size, blk) for x in outs]
    return outs[:pieces], outs[pieces:]


def table_at(cap, q, kind):
    return (q * 3 + kind) * (1 + 2 * cap)


def table_kernel(n, cap, dest, table):
    classes, n_s = dest.shape
    line = n // Y
    d = lax.axis_index("sector")
    z, y = split(d, Y)
    even = (z & 1) == 0

    for i in range(3 * line):
        table[i * (1 + 2 * cap)] = 0
        for slot in range(cap):
            table[i * (1 + 2 * cap) + 1 + slot] = 0
            table[i * (1 + 2 * cap) + 1 + cap + slot] = n_s

    def position(twice):
        m = wrap(lax.shift_right_arithmetic(twice, 1), line)
        return jnp.where(m == 0, line - 1, jnp.where(even, line - 1 - m, m - 1))

    def note(q, kind, j, p):
        at = table_at(cap, q, kind)
        count = table[at]
        table[at + 1 + count] = j
        table[at + 1 + cap + count] = p
        table[at] = count + 1

    for c in range(classes):

        def step(i, _, c=c):
            t, p = split(dest[c, i], n_s)
            k = wrap(t - d, n)
            j = c * n_s + i

            @pl.when((k & 1) == 0)
            def _():
                note(position(k), OWN, j, p)

            @pl.when((k & 1) == 1)
            def _():
                note(position(k - 1 + 2 * y), SEND, j, p)
                note(position(k + 1 - 2 * y), CROSS, j, p)

            return 0

        lax.fori_loop(0, n_s, step, 0)


def make_table(n, cap, dest):
    return pl.pallas_call(
        functools.partial(table_kernel, n, cap),
        out_shape=jax.ShapeDtypeStruct((3 * (n // Y) * (1 + 2 * cap),), jnp.int32),
        in_specs=[SMEM],
        out_specs=SMEM,
        cost_estimate=pl.CostEstimate(flops=4000, bytes_accessed=4000, transcendentals=0),
    )(dest)


def small_call(kernel, outs, table, ins, after=(), scratch=()):
    spare = len(after)

    def body(table, *refs):
        kernel(table, *refs[:len(ins)], *refs[len(ins) + spare:])

    return pl.pallas_call(
        body,
        out_shape=outs,
        in_specs=[SMEM] + [VMEM] * len(ins) + [pl.BlockSpec(memory_space=pl.ANY)] * spare,
        out_specs=[VMEM] * len(outs),
        scratch_shapes=scratch,
        compiler_params=pltpu.CompilerParams(vmem_limit_bytes=16 * 2**20),
        cost_estimate=pl.CostEstimate(flops=0, bytes_accessed=1000, transcendentals=0),
    )(table, *ins, *after)


def pack(cap, qs, table, keep, recv, after):
    _, size, blk = keep.shape

    def kernel(table, keep, recv, *outs):
        for q, out in zip(qs, outs):
            for slot in range(cap):
                j = table[table_at(cap, q, SEND) + 1 + slot]
                out[slot] = keep[j] + recv[j]

    return small_call(kernel, [jax.ShapeDtypeStruct((cap, size, blk), jnp.bfloat16)] * len(qs), table, (keep, recv), after)


def gather(cap, q, n_s, table, keep, recv, crossed, after, dtype=jnp.bfloat16):
    _, size, blk = keep.shape

    def kernel(table, keep, recv, crossed, out, total):
        total[...] = jnp.zeros_like(total)
        at = table_at(cap, q, OWN) + 1
        for slot in range(cap):
            j = table[at + slot]
            total[table[at + cap + slot]] += (keep[j] + recv[j]).astype(jnp.float32)
        at = table_at(cap, q, CROSS) + 1
        for slot in range(cap):
            total[table[at + cap + slot]] += crossed[slot].astype(jnp.float32)
        out[...] = total[:n_s].astype(dtype)

    (out,) = small_call(
        kernel,
        [jax.ShapeDtypeStruct((n_s, size, blk), dtype)],
        table,
        (keep, recv, crossed),
        after,
        [pltpu.VMEM((n_s + 1, size, blk), jnp.float32)],
    )
    return out


def plus(table, a, b, after):
    def kernel(table, a, b, out):
        out[...] = a[...] + b[...]

    (out,) = small_call(kernel, [jax.ShapeDtypeStruct(a.shape, a.dtype)], table, (a, b), after)
    return out


def finish(rows, bases, arrived):
    n_s, size, blk = bases[0].shape
    pieces = len(bases)

    def kernel(rows, *refs):
        out = refs[-1]
        line = lax.broadcasted_iota(jnp.int32, (size, blk), 0) + lax.axis_index("mpo") * (size * pieces)
        for piece in range(pieces):
            for p in range(n_s):
                total = refs[piece][p]
                for part in refs[pieces + piece:-1:pieces]:
                    total += part[p].astype(jnp.float32)
                total = jnp.where(line + piece * size < rows[p], total, 0.0)
                out[p, piece * size:(piece + 1) * size] = total.astype(jnp.bfloat16)

    flat = list(bases) + [x for parts in arrived for x in parts]
    return pl.pallas_call(
        kernel,
        out_shape=jax.ShapeDtypeStruct((n_s, size * pieces, blk), jnp.bfloat16),
        in_specs=[SMEM] + [VMEM] * len(flat),
        out_specs=VMEM,
        compiler_params=pltpu.CompilerParams(vmem_limit_bytes=16 * 2**20),
        cost_estimate=pl.CostEstimate(flops=0, bytes_accessed=1000, transcendentals=0),
    )(rows, *flat)


def body(psi, left_env, right_env, term_class, active, dest, sector_rows):
    n = lax.axis_size("sector")
    line = n // Y
    classes, n_s = dest.shape
    cap = (classes * n_s + n - 1) // n + 1
    pieces = range(2)
    across = [(d, d ^ 1) for d in range(n)]
    near = [(z * Y + y, (z ^ 1) * Y + y) for z in range(line) for y in range(Y)]
    far = [(z * Y + y, (((z + 1) ^ 1) - 1) * Y + y) for z in range(1, line - 1) for y in range(Y)]

    def cross(x):
        return lax.ppermute(x, "sector", across)

    send, keep = shift_sums(psi, left_env, right_env, term_class, active, sector_rows, classes, len(pieces))
    recv = [lax.ppermute(x, "mpo", [(0, 1), (1, 0)]) for x in send]
    table = make_table(n, cap, dest)
    last = ()
    crossed = [[None] * len(pieces) for _ in range(line)]
    for qs in ([0], [1], list(range(2, line))):
        for i in pieces:
            packed = pack(cap, qs, table, keep[i], recv[i], last)
            last = (packed[0],)
            for q, x in zip(qs, packed):
                crossed[q][i] = cross(x)

    acc = [[None] * len(pieces) for _ in range(line)]

    def sums(q, i):
        if acc[q][i] is None:
            dtype = jnp.float32 if q == line - 1 else jnp.bfloat16
            acc[q][i] = gather(cap, q, n_s, table, keep[i], recv[i], crossed[q][i], last, dtype)
        return acc[q][i], (acc[q][i],)

    near_in, far_in = [None] * len(pieces), [None] * len(pieces)
    for step in range(1, line):
        near_out, far_out = [None] * len(pieces), [None] * len(pieces)
        for i in pieces:
            near_out[i], last = sums(step - 1, i)
            if far_in[i] is not None:
                near_out[i] = plus(table, near_out[i], far_in[i], last)
                last = (near_out[i],)
            if step > 1:
                base, last = sums(line - 1 - step, i)
                far_out[i] = plus(table, base, near_in[i], last)
                last = (far_out[i],)
        near_in = [lax.ppermute(x, "sector", near) for x in near_out]
        far_in = [None if x is None else lax.ppermute(x, "sector", far) for x in far_out]
    bases = [sums(line - 1, i)[0] for i in pieces]
    return finish(sector_rows, bases, [x for x in (near_in, far_in) if x[0] is not None])


def solution(mesh):
    placed = (
        P(("groups", "sector"), None, None),
        P(("groups", "mpo"), "sector", None, None),
        P(("groups", "mpo"), "sector", None, None),
        P(("groups", "mpo")),
        P(("groups", "mpo"), "sector"),
        P("groups", "sector"),
        P(("groups", "sector")),
    )
    return jax.shard_map(
        body,
        mesh=mesh,
        in_specs=placed,
        out_specs=P(("groups", "sector"), "mpo", None),
        check_vma=False,
    )
```

```python
import functools

import jax
import jax.numpy as jnp
from jax import lax
from jax.experimental import pallas as pl
from jax.experimental.pallas import tpu as pltpu
from jax.sharding import PartitionSpec as P

SMEM = pl.BlockSpec(memory_space=pltpu.SMEM)
VMEM = pl.BlockSpec(memory_space=pltpu.VMEM)
HBM = pl.BlockSpec(memory_space=pltpu.HBM)
Y = 2
OWN, SEND, CROSS = range(3)


def split(x, by):
    if by & (by - 1) == 0:
        return lax.shift_right_logical(x, by.bit_length() - 1), x & (by - 1)
    return x // by, lax.rem(x, by)


def wrap(x, by):
    x = jnp.where(x < 0, x + by, x)
    return jnp.where(x >= by, x - by, x)


def shifts_kernel(slots, masked, left, right, *refs):
    pieces = (len(refs) - 5) // 2
    send, keep = refs[:pieces], refs[pieces:2 * pieces]
    lbuf, rbuf, inner, acc, sems = refs[2 * pieces:]
    n_w, n_s, blk = right.shape[:3]
    classes, _, size = send[0].shape[:3]
    depth = lbuf.shape[0]
    me = lax.axis_index("mpo")

    def copies(s):
        at = lax.rem(s, depth)
        return (
            pltpu.make_async_copy(left.at[:, s], lbuf.at[at], sems.at[0, at]),
            pltpu.make_async_copy(right.at[:, s], rbuf.at[at], sems.at[1, at]),
        )

    for s in range(min(depth, n_s)):
        for c in copies(jnp.int32(s)):
            c.start()

    def sector(s, _):
        at = lax.rem(s, depth)
        for c in copies(s):
            c.wait()
        for c in range(classes):
            acc[c] = jnp.zeros(acc.shape[1:], jnp.float32)
        for w in range(n_w):
            inner[w * blk:(w + 1) * blk] = jnp.dot(
                lbuf[at, w], masked[s], preferred_element_type=jnp.float32
            ).astype(jnp.bfloat16)
        for w in range(n_w):
            acc[slots[s, w]] += jnp.dot(
                inner[w * blk:(w + 1) * blk], rbuf[at, w], preferred_element_type=jnp.float32
            )

        @pl.when(s + depth < n_s)
        def _():
            for c in copies(s + depth):
                c.start()

        for piece in range(pieces):
            mine = pl.multiple_of(me * (blk // 2) + piece * size, size)
            other = pl.multiple_of((1 - me) * (blk // 2) + piece * size, size)
            for c in range(classes):
                keep[piece][c, s] = acc[c, pl.ds(mine, size), :].astype(jnp.bfloat16)
                send[piece][c, s] = acc[c, pl.ds(other, size), :].astype(jnp.bfloat16)
        return 0

    lax.fori_loop(0, n_s, sector, 0)


def shift_sums(psi, left_env, right_env, term_class, active, sector_rows, classes, pieces):
    n_w, n_s, blk = left_env.shape[:3]
    size = blk // 2 // pieces
    depth = 3
    line = jnp.arange(blk, dtype=jnp.int32)
    masked = jnp.where(line[None, :, None] < sector_rows[:, None, None], psi, jnp.zeros_like(psi))
    slots = jnp.where(active.T == 1, term_class[None, :], classes)
    outs = pl.pallas_call(
        shifts_kernel,
        out_shape=[jax.ShapeDtypeStruct((classes, n_s, size, blk), jnp.bfloat16)] * (2 * pieces),
        in_specs=[SMEM, VMEM, HBM, HBM],
        out_specs=[VMEM] * (2 * pieces),
        scratch_shapes=[
            pltpu.VMEM((depth, n_w, blk, blk), jnp.bfloat16),
            pltpu.VMEM((depth, n_w, blk, blk), jnp.bfloat16),
            pltpu.VMEM((n_w * blk, blk), jnp.bfloat16),
            pltpu.VMEM((classes + 1, blk, blk), jnp.float32),
            pltpu.SemaphoreType.DMA((2, depth)),
        ],
        compiler_params=pltpu.CompilerParams(vmem_limit_bytes=40 * 2**20),
        cost_estimate=pl.CostEstimate(
            flops=4 * n_w * n_s * blk**3, bytes_accessed=4 * n_w * n_s * blk * blk, transcendentals=0
        ),
    )(slots, masked, left_env, right_env)
    outs = [x.reshape(classes * n_s, size, blk) for x in outs]
    return outs[:pieces], outs[pieces:]


def table_at(cap, q, kind):
    return (q * 3 + kind) * (1 + 2 * cap)


def table_kernel(n, cap, dest, table):
    classes, n_s = dest.shape
    line = n // Y
    d = lax.axis_index("sector")
    z, y = split(d, Y)
    even = (z & 1) == 0

    for i in range(3 * line):
        table[i * (1 + 2 * cap)] = 0
        for slot in range(cap):
            table[i * (1 + 2 * cap) + 1 + slot] = 0
            table[i * (1 + 2 * cap) + 1 + cap + slot] = n_s

    def position(twice):
        m = wrap(lax.shift_right_arithmetic(twice, 1), line)
        return jnp.where(m == 0, line - 1, jnp.where(even, line - 1 - m, m - 1))

    def note(q, kind, j, p):
        at = table_at(cap, q, kind)
        count = table[at]
        table[at + 1 + count] = j
        table[at + 1 + cap + count] = p
        table[at] = count + 1

    for c in range(classes):

        def step(i, _, c=c):
            t, p = split(dest[c, i], n_s)
            k = wrap(t - d, n)
            j = c * n_s + i

            @pl.when((k & 1) == 0)
            def _():
                note(position(k), OWN, j, p)

            @pl.when((k & 1) == 1)
            def _():
                note(position(k - 1 + 2 * y), SEND, j, p)
                note(position(k + 1 - 2 * y), CROSS, j, p)

            return 0

        lax.fori_loop(0, n_s, step, 0)


def make_table(n, cap, dest):
    return pl.pallas_call(
        functools.partial(table_kernel, n, cap),
        out_shape=jax.ShapeDtypeStruct((3 * (n // Y) * (1 + 2 * cap),), jnp.int32),
        in_specs=[SMEM],
        out_specs=SMEM,
        compiler_params=pltpu.CompilerParams(vmem_limit_bytes=2**20),
        cost_estimate=pl.CostEstimate(flops=4000, bytes_accessed=4000, transcendentals=0),
    )(dest)


def small_call(kernel, outs, ins, table=None, after=(), scratch=(), cost=1000):
    front = [] if table is None else [table]
    used = len(front) + len(ins)

    def body(*refs):
        kernel(*refs[:used], *refs[used + len(after):])

    return pl.pallas_call(
        body,
        out_shape=outs,
        in_specs=[SMEM] * len(front) + [VMEM] * len(ins) + [pl.BlockSpec(memory_space=pl.ANY)] * len(after),
        out_specs=[VMEM] * len(outs),
        scratch_shapes=scratch,
        compiler_params=pltpu.CompilerParams(vmem_limit_bytes=8 * 2**20),
        cost_estimate=pl.CostEstimate(flops=0, bytes_accessed=cost, transcendentals=0),
    )(*front, *ins, *after)


def ready(table):
    def kernel(table, out):
        out[...] = jnp.full(out.shape, table[0], jnp.int32)

    return small_call(kernel, [jax.ShapeDtypeStruct((8, 128), jnp.int32)], (), table)


def join(cap, table, keep, recv, after):
    _, size, blk = keep.shape

    def kernel(table, keep, recv, joined, out):
        joined[...] = keep[...] + recv[...]
        for slot in range(cap):
            out[slot] = joined[table[table_at(cap, 0, SEND) + 1 + slot]]

    return small_call(
        kernel,
        [keep, jax.ShapeDtypeStruct((cap, size, blk), jnp.bfloat16)],
        (keep, recv),
        table,
        after,
    )


def pack(cap, spots, table, joined, after):
    _, size, blk = joined[0].shape
    used = sorted({i for _, i in spots})

    def kernel(table, *refs):
        out = refs[-1]
        for at, (q, i) in enumerate(spots):
            for slot in range(cap):
                out[at * cap + slot] = refs[used.index(i)][table[table_at(cap, q, SEND) + 1 + slot]]

    (out,) = small_call(
        kernel,
        [jax.ShapeDtypeStruct((len(spots) * cap, size, blk), jnp.bfloat16)],
        [joined[i] for i in used],
        table,
        after,
    )
    return out


def gather(cap, q, pieces, n_s, table, joined, crossed, after, dtype=jnp.bfloat16, cost=1000):
    _, size, blk = joined[0].shape
    count = len(pieces)
    spots = [crossed[q, i] for i in pieces]

    def kernel(table, *refs):
        out, total = refs[-2:]
        for k in range(count):
            a, c = refs[k], refs[count + k]
            total[...] = jnp.zeros_like(total)
            at = table_at(cap, q, OWN) + 1
            for slot in range(cap):
                j = table[at + slot]
                total[table[at + cap + slot]] += a[j].astype(jnp.float32)
            at = table_at(cap, q, CROSS) + 1
            for slot in range(cap):
                total[table[at + cap + slot]] += c[spots[k][1] + slot].astype(jnp.float32)
            out[k * n_s:(k + 1) * n_s] = total[:n_s].astype(dtype)

    (out,) = small_call(
        kernel,
        [jax.ShapeDtypeStruct((count * n_s, size, blk), dtype)],
        [joined[i] for i in pieces] + [x for x, _ in spots],
        table,
        after,
        [pltpu.VMEM((n_s + 1, size, blk), jnp.float32)],
        cost,
    )
    return out


def advance(cap, n_s, line, step, i, table, joined, crossed, acc, near_in, far_in, after):
    size, blk = joined.shape[1:]
    block = jax.ShapeDtypeStruct((n_s, size, blk), jnp.bfloat16)
    sends = [(step - 1, far_in)] + ([(line - 1 - step, near_in)] if step > 1 else [])
    fresh = sorted({q for q, _ in sends if q not in acc})
    ins, at = [joined], {}
    for q in fresh:
        at[q] = len(ins)
        ins.append(crossed[q, i][0])
    for q, arrived in sends:
        if q not in fresh:
            at[q] = len(ins)
            ins.append(acc[q])
    came = []
    for _, arrived in sends:
        came.append(len(ins))
        if arrived is not None:
            ins.append(arrived)
    saved = [q for q in fresh if step < max(q + 1, line - 1 - q) and step > 1]

    def kernel(*refs):
        if fresh:
            table, refs = refs[0], refs[1:]
        totals = refs[len(refs) - len(fresh):]
        outs = refs[len(ins):]
        for total, q in zip(totals, fresh):
            total[...] = jnp.zeros_like(total)
            spot = table_at(cap, q, OWN) + 1
            for slot in range(cap):
                total[table[spot + cap + slot]] += refs[0][table[spot + slot]].astype(jnp.float32)
            spot = table_at(cap, q, CROSS) + 1
            for slot in range(cap):
                total[table[spot + cap + slot]] += refs[at[q]][crossed[q, i][1] + slot].astype(jnp.float32)
        for k, (q, arrived) in enumerate(sends):
            message = totals[fresh.index(q)][:n_s] if q in fresh else refs[at[q]][...].astype(jnp.float32)
            if arrived is not None:
                message += refs[came[k]][...].astype(jnp.float32)
            outs[k][...] = message.astype(jnp.bfloat16)
        for k, q in enumerate(saved):
            outs[len(sends) + k][...] = totals[fresh.index(q)][:n_s].astype(jnp.bfloat16)

    outs = small_call(
        kernel,
        [block] * (len(sends) + len(saved)),
        ins,
        table if fresh else None,
        after,
        [pltpu.VMEM((n_s + 1, size, blk), jnp.float32)] * len(fresh),
    )
    for q, x in zip(saved, outs[len(sends):]):
        acc[q] = x
    if step == 1:
        acc[0] = outs[0]
    return outs[:len(sends)]


def finish(n_s, piece, rows, base, arrived, out=None):
    size, blk = base.shape[1:]
    half = blk // 2

    def kernel(rows, base, *refs):
        parts, (out, held, sem) = refs[:len(arrived)], refs[-3:]
        line = lax.broadcasted_iota(jnp.int32, (size, blk), 0) + (lax.axis_index("mpo") * half + piece * size)
        for p in range(n_s):
            total = base[p]
            for part in parts:
                total += part[p].astype(jnp.float32)
            held[p] = jnp.where(line < rows[p:p + 1], total, 0.0).astype(jnp.bfloat16)
        leave = pltpu.make_async_copy(held, out.at[:, piece * size:(piece + 1) * size], sem)
        leave.start()
        leave.wait()

    ins = [rows, base, *arrived]
    return pl.pallas_call(
        kernel,
        out_shape=jax.ShapeDtypeStruct((n_s, half, blk), jnp.bfloat16),
        in_specs=[VMEM] * len(ins) + ([HBM] if out is not None else []),
        out_specs=HBM,
        scratch_shapes=[pltpu.VMEM((n_s, size, blk), jnp.bfloat16), pltpu.SemaphoreType.DMA],
        input_output_aliases={len(ins): 0} if out is not None else {},
        compiler_params=pltpu.CompilerParams(vmem_limit_bytes=8 * 2**20),
        cost_estimate=pl.CostEstimate(flops=0, bytes_accessed=1000, transcendentals=0),
    )(*ins, *([out] if out is not None else []))


def body(psi, left_env, right_env, term_class, active, dest, sector_rows):
    n = lax.axis_size("sector")
    line = n // Y
    classes, n_s = dest.shape
    cap = (classes * n_s + n - 1) // n + 1
    pieces = [0, 1]
    across = [(d, d ^ 1) for d in range(n)]
    near = [(z * Y + y, (z ^ 1) * Y + y) for z in range(line) for y in range(Y)]
    far = [(z * Y + y, (((z + 1) ^ 1) - 1) * Y + y) for z in range(1, line - 1) for y in range(Y)]

    send, keep = shift_sums(psi, left_env, right_env, term_class, active, sector_rows, classes, len(pieces))
    recv = [lax.ppermute(x, "mpo", [(0, 1), (1, 0)]) for x in send]
    table = make_table(n, cap, dest)

    loads = [[(q, i)] for q in range(line - 1) for i in pieces]
    loads.append([(line - 1, i) for i in pieces])
    crossed, joined, came = {}, [], []
    last = ready(table)
    for k, spots in enumerate(loads):
        if k < len(pieces):
            whole, packed = join(cap, table, keep[k], recv[k], last)
            joined.append(whole)
        else:
            packed = pack(cap, spots, table, joined, last)
        last = [packed]
        if k == 3:
            firsts = packed
        came.append(lax.ppermute(packed, "sector", across))
        for at, spot in enumerate(spots):
            crossed[spot] = (came[k], at * cap)
        if k >= 3:
            last = [packed, came[k - 2]]

    acc = [{} for _ in pieces]
    near_in, far_in = [None for _ in pieces], [None for _ in pieces]
    last = [firsts]
    for step in range(1, line):
        for i in pieces:
            out = advance(cap, n_s, line, step, i, table, joined[i], crossed, acc[i], near_in[i], far_in[i], last)
            last = [out[0]]
            near_in[i] = lax.ppermute(out[0], "sector", near)
            far_in[i] = lax.ppermute(out[1], "sector", far) if step > 1 else None
    limits = jnp.broadcast_to(sector_rows[:, None], (n_s, psi.shape[2]))
    out = None
    for i in pieces:
        base = gather(cap, line - 1, [i], n_s, table, joined, crossed, (), jnp.float32)
        arrived = [x[i] for x in (near_in, far_in) if x[i] is not None]
        out = finish(n_s, i, limits, base, arrived, out)
    return out


def solution(mesh):
    placed = (
        P(("groups", "sector"), None, None),
        P(("groups", "mpo"), "sector", None, None),
        P(("groups", "mpo"), "sector", None, None),
        P(("groups", "mpo")),
        P(("groups", "mpo"), "sector"),
        P("groups", "sector"),
        P(("groups", "sector")),
    )
    return jax.shard_map(
        body,
        mesh=mesh,
        in_specs=placed,
        out_specs=P(("groups", "sector"), "mpo", None),
        check_vma=False,
    )
```

```python
import functools

import jax
import jax.numpy as jnp
from jax import lax
from jax.experimental import pallas as pl
from jax.experimental.pallas import tpu as pltpu
from jax.sharding import PartitionSpec as P

SMEM = pl.BlockSpec(memory_space=pltpu.SMEM)
VMEM = pl.BlockSpec(memory_space=pltpu.VMEM)
HBM = pl.BlockSpec(memory_space=pltpu.HBM)
Y = 2
OWN, SEND, CROSS = range(3)


def split(x, by):
    if by & (by - 1) == 0:
        return lax.shift_right_logical(x, by.bit_length() - 1), x & (by - 1)
    return x // by, lax.rem(x, by)


def wrap(x, by):
    x = jnp.where(x < 0, x + by, x)
    return jnp.where(x >= by, x - by, x)


def shifts_kernel(slots, masked, left, right, *refs):
    pieces = (len(refs) - 5) // 2
    send, keep = refs[:pieces], refs[pieces:2 * pieces]
    lbuf, rbuf, inner, acc, sems = refs[2 * pieces:]
    n_w, n_s, blk = right.shape[:3]
    classes, _, size = send[0].shape[:3]
    depth = lbuf.shape[0]
    me = lax.axis_index("mpo")

    def copies(s):
        at = lax.rem(s, depth)
        return (
            pltpu.make_async_copy(left.at[:, s], lbuf.at[at], sems.at[0, at]),
            pltpu.make_async_copy(right.at[:, s], rbuf.at[at], sems.at[1, at]),
        )

    for s in range(min(depth, n_s)):
        for c in copies(jnp.int32(s)):
            c.start()

    def sector(s, _):
        at = lax.rem(s, depth)
        for c in copies(s):
            c.wait()
        for c in range(classes):
            acc[c] = jnp.zeros(acc.shape[1:], jnp.float32)
        for w in range(n_w):
            inner[w * blk:(w + 1) * blk] = jnp.dot(
                lbuf[at, w], masked[s], preferred_element_type=jnp.float32
            ).astype(jnp.bfloat16)
        for w in range(n_w):
            acc[slots[s, w]] += jnp.dot(
                inner[w * blk:(w + 1) * blk], rbuf[at, w], preferred_element_type=jnp.float32
            )

        @pl.when(s + depth < n_s)
        def _():
            for c in copies(s + depth):
                c.start()

        for piece in range(pieces):
            mine = pl.multiple_of(me * (blk // 2) + piece * size, size)
            other = pl.multiple_of((1 - me) * (blk // 2) + piece * size, size)
            for c in range(classes):
                keep[piece][c, s] = acc[c, pl.ds(mine, size), :].astype(jnp.bfloat16)
                send[piece][c, s] = acc[c, pl.ds(other, size), :].astype(jnp.bfloat16)
        return 0

    lax.fori_loop(0, n_s, sector, 0)


def shift_sums(psi, left_env, right_env, term_class, active, sector_rows, classes, pieces):
    n_w, n_s, blk = left_env.shape[:3]
    size = blk // 2 // pieces
    depth = 3
    line = jnp.arange(blk, dtype=jnp.int32)
    masked = jnp.where(line[None, :, None] < sector_rows[:, None, None], psi, jnp.zeros_like(psi))
    slots = jnp.where(active.T == 1, term_class[None, :], classes)
    outs = pl.pallas_call(
        shifts_kernel,
        out_shape=[jax.ShapeDtypeStruct((classes, n_s, size, blk), jnp.bfloat16)] * (2 * pieces),
        in_specs=[SMEM, VMEM, HBM, HBM],
        out_specs=[VMEM] * (2 * pieces),
        scratch_shapes=[
            pltpu.VMEM((depth, n_w, blk, blk), jnp.bfloat16),
            pltpu.VMEM((depth, n_w, blk, blk), jnp.bfloat16),
            pltpu.VMEM((n_w * blk, blk), jnp.bfloat16),
            pltpu.VMEM((classes + 1, blk, blk), jnp.float32),
            pltpu.SemaphoreType.DMA((2, depth)),
        ],
        compiler_params=pltpu.CompilerParams(vmem_limit_bytes=40 * 2**20),
        cost_estimate=pl.CostEstimate(
            flops=4 * n_w * n_s * blk**3, bytes_accessed=4 * n_w * n_s * blk * blk, transcendentals=0
        ),
    )(slots, masked, left_env, right_env)
    outs = [x.reshape(classes * n_s, size, blk) for x in outs]
    return outs[:pieces], outs[pieces:]


def table_at(cap, q, kind):
    return (q * 3 + kind) * (1 + 2 * cap)


def table_kernel(n, cap, dest, table):
    classes, n_s = dest.shape
    line = n // Y
    spare = 3 * line
    d = lax.axis_index("sector")
    z, y = split(d, Y)
    even = (z & 1) == 0
    for i in range(spare + 1):
        table[i * (1 + 2 * cap)] = 0
        for slot in range(cap):
            table[i * (1 + 2 * cap) + 1 + slot] = 0
            table[i * (1 + 2 * cap) + 1 + cap + slot] = n_s

    def position(twice):
        m = wrap(lax.shift_right_arithmetic(twice, 1), line)
        return jnp.where(m == 0, line - 1, jnp.where(even, line - 1 - m, m - 1))

    def note(which, j, p):
        at = which * (1 + 2 * cap)
        count = table[at]
        table[at + 1 + count] = j
        table[at + 1 + cap + count] = p
        table[at] = count + 1

    for j in range(classes * n_s):
        t, p = split(dest[j // n_s, j % n_s], n_s)
        k = wrap(t - d, n)
        odd = k & 1
        stays = odd == 0
        note(jnp.where(stays, position(k) * 3 + OWN, position(k - 1 + 2 * y) * 3 + SEND), j, p)
        table[spare * (1 + 2 * cap)] = 0
        note(jnp.where(stays, spare, position(k + 1 - 2 * y) * 3 + CROSS), j, p)


def make_table(n, cap, dest):
    return pl.pallas_call(
        functools.partial(table_kernel, n, cap),
        out_shape=jax.ShapeDtypeStruct(((3 * (n // Y) + 1) * (1 + 2 * cap),), jnp.int32),
        in_specs=[SMEM],
        out_specs=SMEM,
        compiler_params=pltpu.CompilerParams(vmem_limit_bytes=2**20),
        cost_estimate=pl.CostEstimate(flops=4000, bytes_accessed=4000, transcendentals=0),
    )(dest)


def small_call(kernel, outs, ins, table=None, after=(), scratch=(), cost=1000):
    front = [] if table is None else [table]
    used = len(front) + len(ins)

    def body(*refs):
        kernel(*refs[:used], *refs[used + len(after):])

    return pl.pallas_call(
        body,
        out_shape=outs,
        in_specs=[SMEM] * len(front) + [VMEM] * len(ins) + [pl.BlockSpec(memory_space=pl.ANY)] * len(after),
        out_specs=[VMEM] * len(outs),
        scratch_shapes=scratch,
        compiler_params=pltpu.CompilerParams(vmem_limit_bytes=8 * 2**20),
        cost_estimate=pl.CostEstimate(flops=0, bytes_accessed=cost, transcendentals=0),
    )(*front, *ins, *after)


def ready(table):
    def kernel(table, out):
        out[...] = jnp.full(out.shape, table[0], jnp.int32)

    return small_call(kernel, [jax.ShapeDtypeStruct((8, 128), jnp.int32)], (), table)


def join(cap, table, keep, recv, after):
    _, size, blk = keep.shape

    def kernel(table, keep, recv, joined, out):
        joined[...] = keep[...] + recv[...]
        for slot in range(cap):
            out[slot] = joined[table[table_at(cap, 0, SEND) + 1 + slot]]

    return small_call(
        kernel,
        [keep, jax.ShapeDtypeStruct((cap, size, blk), jnp.bfloat16)],
        (keep, recv),
        table,
        after,
    )


def pack(cap, loads, table, joined, after):
    _, size, blk = joined[0].shape
    used = sorted({i for spots in loads for _, i in spots})

    def kernel(table, *refs):
        for spots, out in zip(loads, refs[len(used):]):
            for at, (q, i) in enumerate(spots):
                for slot in range(cap):
                    out[at * cap + slot] = refs[used.index(i)][table[table_at(cap, q, SEND) + 1 + slot]]

    return small_call(
        kernel,
        [jax.ShapeDtypeStruct((len(spots) * cap, size, blk), jnp.bfloat16) for spots in loads],
        [joined[i] for i in used],
        table,
        after,
    )


def has_far(line):
    z, _ = split(lax.axis_index("sector"), Y)
    return (z > 0) & (z < line - 1)


def gather(cap, q, pieces, n_s, table, joined, crossed, after, dtype=jnp.bfloat16, cost=1000):
    _, size, blk = joined[0].shape
    count = len(pieces)
    spots = [crossed[q, i] for i in pieces]

    def kernel(table, *refs):
        out, total = refs[-2:]
        for k in range(count):
            a, c = refs[k], refs[count + k]
            total[...] = jnp.zeros_like(total)
            at = table_at(cap, q, OWN) + 1
            for slot in range(cap):
                j = table[at + slot]
                total[table[at + cap + slot]] += a[j].astype(jnp.float32)
            at = table_at(cap, q, CROSS) + 1
            for slot in range(cap):
                total[table[at + cap + slot]] += c[spots[k][1] + slot].astype(jnp.float32)
            out[k * n_s:(k + 1) * n_s] = total[:n_s].astype(dtype)

    (out,) = small_call(
        kernel,
        [jax.ShapeDtypeStruct((count * n_s, size, blk), dtype)],
        [joined[i] for i in pieces] + [x for x, _ in spots],
        table,
        after,
        [pltpu.VMEM((n_s + 1, size, blk), jnp.float32)],
        cost,
    )
    return out


def advance(cap, n_s, line, step, i, table, joined, crossed, acc, near_in, far_in, after):
    size, blk = joined.shape[1:]
    block = jax.ShapeDtypeStruct((n_s, size, blk), jnp.bfloat16)
    sends = [(step - 1, far_in)] + ([(line - 1 - step, near_in)] if step > 1 else [])
    fresh = sorted({q for q, _ in sends if q not in acc})
    ins, at = [joined], {}
    for q in fresh:
        at[q] = len(ins)
        ins.append(crossed[q, i][0])
    for q, arrived in sends:
        if q not in fresh:
            at[q] = len(ins)
            ins.append(acc[q])
    came = []
    for _, arrived in sends:
        came.append(len(ins))
        if arrived is not None:
            ins.append(arrived)
    saved = [q for q in fresh if step < max(q + 1, line - 1 - q) and step > 1]

    def kernel(*refs):
        if fresh:
            table, refs = refs[0], refs[1:]
        totals = refs[len(refs) - len(fresh):]
        outs = refs[len(ins):]
        for total, q in zip(totals, fresh):
            total[...] = jnp.zeros_like(total)
            spot = table_at(cap, q, OWN) + 1
            for slot in range(cap):
                total[table[spot + cap + slot]] += refs[0][table[spot + slot]].astype(jnp.float32)
            spot = table_at(cap, q, CROSS) + 1
            for slot in range(cap):
                total[table[spot + cap + slot]] += refs[at[q]][crossed[q, i][1] + slot].astype(jnp.float32)
        for k, (q, arrived) in enumerate(sends):
            message = totals[fresh.index(q)][:n_s] if q in fresh else refs[at[q]][...].astype(jnp.float32)
            if arrived is not None:
                extra = refs[came[k]][...].astype(jnp.float32)
                message += jnp.where(has_far(line), extra, 0.0) if k == 0 else extra
            outs[k][...] = message.astype(jnp.bfloat16)
        for k, q in enumerate(saved):
            outs[len(sends) + k][...] = totals[fresh.index(q)][:n_s].astype(jnp.bfloat16)

    outs = small_call(
        kernel,
        [block] * (len(sends) + len(saved)),
        ins,
        table if fresh else None,
        after,
        [pltpu.VMEM((n_s + 1, size, blk), jnp.float32)] * len(fresh),
    )
    for q, x in zip(saved, outs[len(sends):]):
        acc[q] = x
    if step == 1:
        acc[0] = outs[0]
    return outs[:len(sends)]


def finish(n_s, line, piece, rows, base, arrived, out=None):
    size, blk = base.shape[1:]
    half = blk // 2

    def kernel(rows, base, *refs):
        parts, (out, held, sem) = refs[:len(arrived)], refs[-3:]
        row = lax.broadcasted_iota(jnp.int32, (size, blk), 0) + (lax.axis_index("mpo") * half + piece * size)
        inner = has_far(line)
        for p in range(n_s):
            total = base[p] + parts[0][p].astype(jnp.float32)
            for part in parts[1:]:
                total += jnp.where(inner, part[p].astype(jnp.float32), 0.0)
            held[p] = jnp.where(row < rows[p:p + 1], total, 0.0).astype(jnp.bfloat16)
        leave = pltpu.make_async_copy(held, out.at[:, piece * size:(piece + 1) * size], sem)
        leave.start()
        leave.wait()

    ins = [rows, base, *arrived]
    return pl.pallas_call(
        kernel,
        out_shape=jax.ShapeDtypeStruct((n_s, half, blk), jnp.bfloat16),
        in_specs=[VMEM] * len(ins) + ([HBM] if out is not None else []),
        out_specs=HBM,
        scratch_shapes=[pltpu.VMEM((n_s, size, blk), jnp.bfloat16), pltpu.SemaphoreType.DMA],
        input_output_aliases={len(ins): 0} if out is not None else {},
        compiler_params=pltpu.CompilerParams(vmem_limit_bytes=8 * 2**20),
        cost_estimate=pl.CostEstimate(flops=0, bytes_accessed=1000, transcendentals=0),
    )(*ins, *([out] if out is not None else []))


def body(psi, left_env, right_env, term_class, active, dest, sector_rows):
    n = lax.axis_size("sector")
    line = n // Y
    classes, n_s = dest.shape
    cap = (classes * n_s + n - 1) // n + 1
    pieces = [0, 1]
    across = [(d, d ^ 1) for d in range(n)]
    near = [(z * Y + y, (z ^ 1) * Y + y) for z in range(line) for y in range(Y)]
    far = []
    for z in range(line):
        inner = 0 < z < line - 1
        for d in range(z * Y, (z + 1) * Y):
            other = ((((z + 1) ^ 1) - 1) * Y + d % Y) if inner else d
            far += [(d * 2 + core, other * 2 + (core if inner else 1 - core)) for core in range(2)]

    send, keep = shift_sums(psi, left_env, right_env, term_class, active, sector_rows, classes, len(pieces))
    recv = [lax.ppermute(x, "mpo", [(0, 1), (1, 0)]) for x in send]
    table = make_table(n, cap, dest)

    loads = [[(q, i)] for q in range(line - 1) for i in pieces]
    loads.append([(line - 1, i) for i in pieces])
    crossed, joined, came = {}, [], []
    last = ready(table)
    packed = []
    for i in pieces:
        whole, first = join(cap, table, keep[i], recv[i], last)
        joined.append(whole)
        packed.append(first)
        last = [first]
    came = [lax.ppermute(x, "sector", across) for x in packed]
    firsts = pack(cap, loads[2:4], table, joined, last)
    came += [lax.ppermute(x, "sector", across) for x in firsts]
    came += [lax.ppermute(x, "sector", across) for x in pack(cap, loads[4:], table, joined, [firsts[0], came[1]])]
    for spots, x in zip(loads, came):
        for at, spot in enumerate(spots):
            crossed[spot] = (x, at * cap)

    acc = [{} for _ in pieces]
    near_in, far_in = [None for _ in pieces], [None for _ in pieces]
    last = [firsts[0]]
    for step in range(1, line):
        for i in pieces:
            out = advance(cap, n_s, line, step, i, table, joined[i], crossed, acc[i], near_in[i], far_in[i], last)
            last = [out[0]]
            near_in[i] = lax.ppermute(out[0], "sector", near)
            far_in[i] = lax.ppermute(out[1], ("sector", "mpo"), far) if step > 1 else None
    limits = jnp.broadcast_to(sector_rows[:, None], (n_s, psi.shape[2]))
    out = None
    for i in pieces:
        base = gather(cap, line - 1, [i], n_s, table, joined, crossed, (), jnp.float32)
        arrived = [x[i] for x in (near_in, far_in) if x[i] is not None]
        out = finish(n_s, line, i, limits, base, arrived, out)
    return out


def solution(mesh):
    placed = (
        P(("groups", "sector"), None, None),
        P(("groups", "mpo"), "sector", None, None),
        P(("groups", "mpo"), "sector", None, None),
        P(("groups", "mpo")),
        P(("groups", "mpo"), "sector"),
        P("groups", "sector"),
        P(("groups", "sector")),
    )
    return jax.shard_map(
        body,
        mesh=mesh,
        in_specs=placed,
        out_specs=P(("groups", "sector"), "mpo", None),
        check_vma=False,
    )
```

```python
import functools

import jax
import jax.numpy as jnp
from jax import lax
from jax.experimental import pallas as pl
from jax.experimental.pallas import tpu as pltpu
from jax.sharding import PartitionSpec as P

SMEM = pl.BlockSpec(memory_space=pltpu.SMEM)
VMEM = pl.BlockSpec(memory_space=pltpu.VMEM)
HBM = pl.BlockSpec(memory_space=pltpu.HBM)
Y = 2
OWN, SEND, CROSS = range(3)


def split(x, by):
    if by & (by - 1) == 0:
        return lax.shift_right_logical(x, by.bit_length() - 1), x & (by - 1)
    return x // by, lax.rem(x, by)


def wrap(x, by):
    x = jnp.where(x < 0, x + by, x)
    return jnp.where(x >= by, x - by, x)


def shifts_kernel(slots, masked, left, right, *refs):
    pieces = (len(refs) - 5) // 2
    send, keep = refs[:pieces], refs[pieces:2 * pieces]
    lbuf, rbuf, inner, acc, sems = refs[2 * pieces:]
    n_w, n_s, blk = right.shape[:3]
    classes, _, size = send[0].shape[:3]
    depth = lbuf.shape[0]
    me = lax.axis_index("mpo")

    def copies(s):
        at = lax.rem(s, depth)
        return (
            pltpu.make_async_copy(left.at[:, s], lbuf.at[at], sems.at[0, at]),
            pltpu.make_async_copy(right.at[:, s], rbuf.at[at], sems.at[1, at]),
        )

    for s in range(min(depth, n_s)):
        for c in copies(jnp.int32(s)):
            c.start()

    def sector(s, _):
        at = lax.rem(s, depth)
        for c in copies(s):
            c.wait()
        for c in range(classes):
            acc[c] = jnp.zeros(acc.shape[1:], jnp.float32)
        for w in range(n_w):
            inner[w * blk:(w + 1) * blk] = jnp.dot(
                lbuf[at, w], masked[s], preferred_element_type=jnp.float32
            ).astype(jnp.bfloat16)
        for w in range(n_w):
            acc[slots[s, w]] += jnp.dot(
                inner[w * blk:(w + 1) * blk], rbuf[at, w], preferred_element_type=jnp.float32
            )

        @pl.when(s + depth < n_s)
        def _():
            for c in copies(s + depth):
                c.start()

        for piece in range(pieces):
            mine = pl.multiple_of(me * (blk // 2) + piece * size, size)
            other = pl.multiple_of((1 - me) * (blk // 2) + piece * size, size)
            for c in range(classes):
                keep[piece][c, s] = acc[c, pl.ds(mine, size), :].astype(jnp.bfloat16)
                send[piece][c, s] = acc[c, pl.ds(other, size), :].astype(jnp.bfloat16)
        return 0

    lax.fori_loop(0, n_s, sector, 0)


def shift_sums(psi, left_env, right_env, term_class, active, sector_rows, classes, pieces):
    n_w, n_s, blk = left_env.shape[:3]
    size = blk // 2 // pieces
    depth = 4
    line = lax.broadcasted_iota(jnp.int32, psi.shape, 1)
    masked = jnp.where(line < lax.broadcast_in_dim(sector_rows, psi.shape, (0,)), psi, jnp.zeros_like(psi))
    slots = jnp.where(active.T == 1, term_class[None, :], classes)
    outs = pl.pallas_call(
        shifts_kernel,
        out_shape=[jax.ShapeDtypeStruct((classes, n_s, size, blk), jnp.bfloat16)] * (2 * pieces),
        in_specs=[SMEM, VMEM, HBM, HBM],
        out_specs=[VMEM] * (2 * pieces),
        scratch_shapes=[
            pltpu.VMEM((depth, n_w, blk, blk), jnp.bfloat16),
            pltpu.VMEM((depth, n_w, blk, blk), jnp.bfloat16),
            pltpu.VMEM((n_w * blk, blk), jnp.bfloat16),
            pltpu.VMEM((classes + 1, blk, blk), jnp.float32),
            pltpu.SemaphoreType.DMA((2, depth)),
        ],
        compiler_params=pltpu.CompilerParams(vmem_limit_bytes=40 * 2**20),
        cost_estimate=pl.CostEstimate(
            flops=4 * n_w * n_s * blk**3, bytes_accessed=4 * n_w * n_s * blk * blk, transcendentals=0
        ),
    )(slots, masked, left_env, right_env)
    outs = [x.reshape(classes * n_s, size, blk) for x in outs]
    return outs[:pieces], outs[pieces:]


def table_at(cap, q, kind):
    return (q * 3 + kind) * (1 + 2 * cap)


def table_kernel(n, cap, dest, table):
    classes, n_s = dest.shape
    line = n // Y
    spare = 3 * line
    d = lax.axis_index("sector")
    z, y = split(d, Y)
    even = (z & 1) == 0
    for i in range(spare + 1):
        table[i * (1 + 2 * cap)] = 0
        for slot in range(cap):
            table[i * (1 + 2 * cap) + 1 + slot] = 0
            table[i * (1 + 2 * cap) + 1 + cap + slot] = n_s

    def position(twice):
        m = wrap(lax.shift_right_arithmetic(twice, 1), line)
        return jnp.where(m == 0, line - 1, jnp.where(even, line - 1 - m, m - 1))

    def note(which, j, p):
        at = which * (1 + 2 * cap)
        count = table[at]
        table[at + 1 + count] = j
        table[at + 1 + cap + count] = p
        table[at] = count + 1

    for j in range(classes * n_s):
        t, p = split(dest[j // n_s, j % n_s], n_s)
        k = wrap(t - d, n)
        odd = k & 1
        stays = odd == 0
        note(jnp.where(stays, position(k) * 3 + OWN, position(k - 1 + 2 * y) * 3 + SEND), j, p)
        table[spare * (1 + 2 * cap)] = 0
        note(jnp.where(stays, spare, position(k + 1 - 2 * y) * 3 + CROSS), j, p)


def make_table(n, cap, dest):
    return pl.pallas_call(
        functools.partial(table_kernel, n, cap),
        out_shape=jax.ShapeDtypeStruct(((3 * (n // Y) + 1) * (1 + 2 * cap),), jnp.int32),
        in_specs=[SMEM],
        out_specs=SMEM,
        compiler_params=pltpu.CompilerParams(vmem_limit_bytes=2**20),
        cost_estimate=pl.CostEstimate(flops=4000, bytes_accessed=4000, transcendentals=0),
    )(dest)


def small_call(kernel, outs, ins, table=None, after=(), scratch=(), cost=1000):
    front = [] if table is None else [table]
    used = len(front) + len(ins)

    def body(*refs):
        kernel(*refs[:used], *refs[used + len(after):])

    return pl.pallas_call(
        body,
        out_shape=outs,
        in_specs=[SMEM] * len(front) + [VMEM] * len(ins) + [pl.BlockSpec(memory_space=pl.ANY)] * len(after),
        out_specs=[VMEM] * len(outs),
        scratch_shapes=scratch,
        compiler_params=pltpu.CompilerParams(vmem_limit_bytes=8 * 2**20),
        cost_estimate=pl.CostEstimate(flops=0, bytes_accessed=cost, transcendentals=0),
    )(*front, *ins, *after)


def ready(table):
    def kernel(table, out):
        out[...] = jnp.full(out.shape, table[0], jnp.int32)

    return small_call(kernel, [jax.ShapeDtypeStruct((8, 128), jnp.int32)], (), table)


def join(cap, table, keep, recv, after):
    _, size, blk = keep.shape

    def kernel(table, keep, recv, joined, out):
        joined[...] = keep[...] + recv[...]
        for slot in range(cap):
            out[slot] = joined[table[table_at(cap, 0, SEND) + 1 + slot]]

    return small_call(
        kernel,
        [keep, jax.ShapeDtypeStruct((cap, size, blk), jnp.bfloat16)],
        (keep, recv),
        table,
        after,
    )


def pack(cap, loads, table, joined, after):
    _, size, blk = joined[0].shape
    used = sorted({i for spots in loads for _, i in spots})

    def kernel(table, *refs):
        for spots, out in zip(loads, refs[len(used):]):
            for at, (q, i) in enumerate(spots):
                for slot in range(cap):
                    out[at * cap + slot] = refs[used.index(i)][table[table_at(cap, q, SEND) + 1 + slot]]

    return small_call(
        kernel,
        [jax.ShapeDtypeStruct((len(spots) * cap, size, blk), jnp.bfloat16) for spots in loads],
        [joined[i] for i in used],
        table,
        after,
    )


def has_far(line):
    z, _ = split(lax.axis_index("sector"), Y)
    return (z > 0) & (z < line - 1)


def gather(cap, q, pieces, n_s, table, joined, crossed, after, dtype=jnp.bfloat16, cost=1000):
    _, size, blk = joined[0].shape
    count = len(pieces)
    spots = [crossed[q, i] for i in pieces]

    def kernel(table, *refs):
        out, total = refs[-2:]
        for k in range(count):
            a, c = refs[k], refs[count + k]
            total[...] = jnp.zeros_like(total)
            at = table_at(cap, q, OWN) + 1
            for slot in range(cap):
                j = table[at + slot]
                total[table[at + cap + slot]] += a[j].astype(jnp.float32)
            at = table_at(cap, q, CROSS) + 1
            for slot in range(cap):
                total[table[at + cap + slot]] += c[spots[k][1] + slot].astype(jnp.float32)
            out[k * n_s:(k + 1) * n_s] = total[:n_s].astype(dtype)

    (out,) = small_call(
        kernel,
        [jax.ShapeDtypeStruct((count * n_s, size, blk), dtype)],
        [joined[i] for i in pieces] + [x for x, _ in spots],
        table,
        after,
        [pltpu.VMEM((n_s + 1, size, blk), jnp.float32)],
        cost,
    )
    return out


def advance(cap, n_s, line, step, i, table, joined, crossed, acc, near_in, far_in, after):
    size, blk = joined.shape[1:]
    block = jax.ShapeDtypeStruct((n_s, size, blk), jnp.bfloat16)
    sends = [(step - 1, far_in)] + ([(line - 1 - step, near_in)] if step > 1 else [])
    fresh = sorted({q for q, _ in sends if q not in acc})
    ins, at = [joined], {}
    for q in fresh:
        at[q] = len(ins)
        ins.append(crossed[q, i][0])
    for q, arrived in sends:
        if q not in fresh:
            at[q] = len(ins)
            ins.append(acc[q])
    came = []
    for _, arrived in sends:
        came.append(len(ins))
        if arrived is not None:
            ins.append(arrived)
    saved = [q for q in fresh if step < max(q + 1, line - 1 - q) and step > 1]

    def kernel(*refs):
        if fresh:
            table, refs = refs[0], refs[1:]
        totals = refs[len(refs) - len(fresh):]
        outs = refs[len(ins):]
        for total, q in zip(totals, fresh):
            total[...] = jnp.zeros_like(total)
            spot = table_at(cap, q, OWN) + 1
            for slot in range(cap):
                total[table[spot + cap + slot]] += refs[0][table[spot + slot]].astype(jnp.float32)
            spot = table_at(cap, q, CROSS) + 1
            for slot in range(cap):
                total[table[spot + cap + slot]] += refs[at[q]][crossed[q, i][1] + slot].astype(jnp.float32)
        for k, (q, arrived) in enumerate(sends):
            message = totals[fresh.index(q)][:n_s] if q in fresh else refs[at[q]][...].astype(jnp.float32)
            if arrived is not None:
                extra = refs[came[k]][...].astype(jnp.float32)
                message += jnp.where(has_far(line), extra, 0.0) if k == 0 else extra
            outs[k][...] = message.astype(jnp.bfloat16)
        for k, q in enumerate(saved):
            outs[len(sends) + k][...] = totals[fresh.index(q)][:n_s].astype(jnp.bfloat16)

    outs = small_call(
        kernel,
        [block] * (len(sends) + len(saved)),
        ins,
        table if fresh else None,
        after,
        [pltpu.VMEM((n_s + 1, size, blk), jnp.float32)] * len(fresh),
    )
    for q, x in zip(saved, outs[len(sends):]):
        acc[q] = x
    if step == 1:
        acc[0] = outs[0]
    return outs[:len(sends)]


def finish(n_s, line, piece, rows, base, arrived, out=None):
    size, blk = base.shape[1:]
    half = blk // 2

    def kernel(rows, base, *refs):
        parts, (out, held, sem) = refs[:len(arrived)], refs[-3:]
        row = lax.broadcasted_iota(jnp.int32, (size, blk), 0) + (lax.axis_index("mpo") * half + piece * size)
        inner = has_far(line)
        for p in range(n_s):
            total = base[p] + parts[0][p].astype(jnp.float32)
            for part in parts[1:]:
                total += jnp.where(inner, part[p].astype(jnp.float32), 0.0)
            held[p] = jnp.where(row < rows[p:p + 1], total, 0.0).astype(jnp.bfloat16)
        leave = pltpu.make_async_copy(held, out.at[:, piece * size:(piece + 1) * size], sem)
        leave.start()
        leave.wait()

    ins = [rows, base, *arrived]
    return pl.pallas_call(
        kernel,
        out_shape=jax.ShapeDtypeStruct((n_s, half, blk), jnp.bfloat16),
        in_specs=[VMEM] * len(ins) + ([HBM] if out is not None else []),
        out_specs=HBM,
        scratch_shapes=[pltpu.VMEM((n_s, size, blk), jnp.bfloat16), pltpu.SemaphoreType.DMA],
        input_output_aliases={len(ins): 0} if out is not None else {},
        compiler_params=pltpu.CompilerParams(vmem_limit_bytes=8 * 2**20),
        cost_estimate=pl.CostEstimate(flops=0, bytes_accessed=1000, transcendentals=0),
    )(*ins, *([out] if out is not None else []))


def body(psi, left_env, right_env, term_class, active, dest, sector_rows):
    n = lax.axis_size("sector")
    line = n // Y
    classes, n_s = dest.shape
    cap = (classes * n_s + n - 1) // n + 1
    pieces = [0, 1]
    across = [(d, d ^ 1) for d in range(n)]
    near = [(z * Y + y, (z ^ 1) * Y + y) for z in range(line) for y in range(Y)]
    far = []
    for z in range(line):
        inner = 0 < z < line - 1
        for d in range(z * Y, (z + 1) * Y):
            other = ((((z + 1) ^ 1) - 1) * Y + d % Y) if inner else d
            far += [(d * 2 + core, other * 2 + (core if inner else 1 - core)) for core in range(2)]

    send, keep = shift_sums(psi, left_env, right_env, term_class, active, sector_rows, classes, len(pieces))
    recv = [lax.ppermute(x, "mpo", [(0, 1), (1, 0)]) for x in send]
    table = make_table(n, cap, dest)

    loads = [[(q, i)] for q in range(line - 1) for i in pieces]
    loads.append([(line - 1, i) for i in pieces])
    crossed, joined, came = {}, [], []
    last = ready(table)
    packed = []
    for i in pieces:
        whole, first = join(cap, table, keep[i], recv[i], last)
        joined.append(whole)
        packed.append(first)
        last = [first]
    came = [lax.ppermute(x, "sector", across) for x in packed]
    firsts = pack(cap, loads[2:4], table, joined, last)
    came += [lax.ppermute(x, "sector", across) for x in firsts]
    came += [lax.ppermute(x, "sector", across) for x in pack(cap, loads[4:], table, joined, [firsts[0], came[1]])]
    for spots, x in zip(loads, came):
        for at, spot in enumerate(spots):
            crossed[spot] = (x, at * cap)

    acc = [{} for _ in pieces]
    near_in, far_in = [None for _ in pieces], [None for _ in pieces]
    last = [firsts[0]]
    for step in range(1, line):
        for i in pieces:
            out = advance(cap, n_s, line, step, i, table, joined[i], crossed, acc[i], near_in[i], far_in[i], last)
            last = [out[0]]
            near_in[i] = lax.ppermute(out[0], "sector", near)
            far_in[i] = lax.ppermute(out[1], ("sector", "mpo"), far) if step > 1 else None
    limits = jnp.broadcast_to(sector_rows[:, None], (n_s, psi.shape[2]))
    out = None
    for i in pieces:
        base = gather(cap, line - 1, [i], n_s, table, joined, crossed, (), jnp.float32)
        arrived = [x[i] for x in (near_in, far_in) if x[i] is not None]
        out = finish(n_s, line, i, limits, base, arrived, out)
    return out


def solution(mesh):
    placed = (
        P(("groups", "sector"), None, None),
        P(("groups", "mpo"), "sector", None, None),
        P(("groups", "mpo"), "sector", None, None),
        P(("groups", "mpo")),
        P(("groups", "mpo"), "sector"),
        P("groups", "sector"),
        P(("groups", "sector")),
    )
    return jax.shard_map(
        body,
        mesh=mesh,
        in_specs=placed,
        out_specs=P(("groups", "sector"), "mpo", None),
        check_vma=False,
    )
```

```python
import functools

import jax
import jax.numpy as jnp
from jax import lax
from jax.experimental import pallas as pl
from jax.experimental.pallas import tpu as pltpu
from jax.sharding import PartitionSpec as P

SMEM = pl.BlockSpec(memory_space=pltpu.SMEM)
VMEM = pl.BlockSpec(memory_space=pltpu.VMEM)
HBM = pl.BlockSpec(memory_space=pltpu.HBM)
Y = 2
OWN, SEND, CROSS = range(3)


def split(x, by):
    if by & (by - 1) == 0:
        return lax.shift_right_logical(x, by.bit_length() - 1), x & (by - 1)
    return x // by, lax.rem(x, by)


def wrap(x, by):
    x = jnp.where(x < 0, x + by, x)
    return jnp.where(x >= by, x - by, x)


def shifts_kernel(slots, masked, left, right, *refs):
    pieces = (len(refs) - 5) // 2
    send, keep = refs[:pieces], refs[pieces:2 * pieces]
    lbuf, rbuf, inner, acc, sems = refs[2 * pieces:]
    n_w, n_s, blk = right.shape[:3]
    classes, _, size = send[0].shape[:3]
    depth = lbuf.shape[0]
    me = lax.axis_index("mpo")

    def copies(s):
        at = lax.rem(s, depth)
        return (
            pltpu.make_async_copy(left.at[:, s], lbuf.at[at], sems.at[0, at]),
            pltpu.make_async_copy(right.at[:, s], rbuf.at[at], sems.at[1, at]),
        )

    for s in range(min(depth, n_s)):
        for c in copies(jnp.int32(s)):
            c.start()

    def sector(s, _):
        at = lax.rem(s, depth)
        for c in copies(s):
            c.wait()
        for c in range(classes):
            acc[c] = jnp.zeros(acc.shape[1:], jnp.float32)
        for w in range(n_w):
            inner[w * blk:(w + 1) * blk] = jnp.dot(
                lbuf[at, w], masked[s], preferred_element_type=jnp.float32
            ).astype(jnp.bfloat16)
        for w in range(n_w):
            acc[slots[s, w]] += jnp.dot(
                inner[w * blk:(w + 1) * blk], rbuf[at, w], preferred_element_type=jnp.float32
            )

        @pl.when(s + depth < n_s)
        def _():
            for c in copies(s + depth):
                c.start()

        for piece in range(pieces):
            mine = pl.multiple_of(me * (blk // 2) + piece * size, size)
            other = pl.multiple_of((1 - me) * (blk // 2) + piece * size, size)
            for c in range(classes):
                keep[piece][c, s] = acc[c, pl.ds(mine, size), :].astype(jnp.bfloat16)
                send[piece][c, s] = acc[c, pl.ds(other, size), :].astype(jnp.bfloat16)
        return 0

    lax.fori_loop(0, n_s, sector, 0)


def shift_sums(psi, left_env, right_env, term_class, active, sector_rows, classes, pieces):
    n_w, n_s, blk = left_env.shape[:3]
    size = blk // 2 // pieces
    depth = 4
    line = lax.broadcasted_iota(jnp.int32, psi.shape, 1)
    masked = jnp.where(line < lax.broadcast_in_dim(sector_rows, psi.shape, (0,)), psi, jnp.zeros_like(psi))
    slots = jnp.where(active.T == 1, term_class[None, :], classes)
    outs = pl.pallas_call(
        shifts_kernel,
        out_shape=[jax.ShapeDtypeStruct((classes, n_s, size, blk), jnp.bfloat16)] * (2 * pieces),
        in_specs=[SMEM, VMEM, HBM, HBM],
        out_specs=[VMEM] * (2 * pieces),
        scratch_shapes=[
            pltpu.VMEM((depth, n_w, blk, blk), jnp.bfloat16),
            pltpu.VMEM((depth, n_w, blk, blk), jnp.bfloat16),
            pltpu.VMEM((n_w * blk, blk), jnp.bfloat16),
            pltpu.VMEM((classes + 1, blk, blk), jnp.float32),
            pltpu.SemaphoreType.DMA((2, depth)),
        ],
        compiler_params=pltpu.CompilerParams(vmem_limit_bytes=40 * 2**20),
        cost_estimate=pl.CostEstimate(
            flops=4 * n_w * n_s * blk**3, bytes_accessed=4 * n_w * n_s * blk * blk, transcendentals=0
        ),
    )(slots, masked, left_env, right_env)
    outs = [x.reshape(classes * n_s, size, blk) for x in outs]
    return outs[:pieces], outs[pieces:]


def table_at(cap, q, kind):
    return (q * 3 + kind) * (1 + 2 * cap)


def table_kernel(n, cap, dest, table):
    classes, n_s = dest.shape
    line = n // Y
    spare = 3 * line
    d = lax.axis_index("sector")
    z, y = split(d, Y)
    even = (z & 1) == 0
    for i in range(spare + 1):
        table[i * (1 + 2 * cap)] = 0
        for slot in range(cap):
            table[i * (1 + 2 * cap) + 1 + slot] = 0
            table[i * (1 + 2 * cap) + 1 + cap + slot] = n_s

    def position(twice):
        m = wrap(lax.shift_right_arithmetic(twice, 1), line)
        return jnp.where(m == 0, line - 1, jnp.where(even, line - 1 - m, m - 1))

    def note(which, j, p):
        at = which * (1 + 2 * cap)
        count = table[at]
        table[at + 1 + count] = j
        table[at + 1 + cap + count] = p
        table[at] = count + 1

    for j in range(classes * n_s):
        t, p = split(dest[j // n_s, j % n_s], n_s)
        k = wrap(t - d, n)
        odd = k & 1
        stays = odd == 0
        note(jnp.where(stays, position(k) * 3 + OWN, position(k - 1 + 2 * y) * 3 + SEND), j, p)
        table[spare * (1 + 2 * cap)] = 0
        note(jnp.where(stays, spare, position(k + 1 - 2 * y) * 3 + CROSS), j, p)


def make_table(n, cap, dest):
    return pl.pallas_call(
        functools.partial(table_kernel, n, cap),
        out_shape=jax.ShapeDtypeStruct(((3 * (n // Y) + 1) * (1 + 2 * cap),), jnp.int32),
        in_specs=[SMEM],
        out_specs=SMEM,
        compiler_params=pltpu.CompilerParams(vmem_limit_bytes=2**20),
        cost_estimate=pl.CostEstimate(flops=4000, bytes_accessed=4000, transcendentals=0),
    )(dest)


def small_call(kernel, outs, ins, table=None, after=(), scratch=(), cost=1000):
    front = [] if table is None else [table]
    used = len(front) + len(ins)

    def body(*refs):
        kernel(*refs[:used], *refs[used + len(after):])

    return pl.pallas_call(
        body,
        out_shape=outs,
        in_specs=[SMEM] * len(front) + [VMEM] * len(ins) + [pl.BlockSpec(memory_space=pl.ANY)] * len(after),
        out_specs=[VMEM] * len(outs),
        scratch_shapes=scratch,
        compiler_params=pltpu.CompilerParams(vmem_limit_bytes=8 * 2**20),
        cost_estimate=pl.CostEstimate(flops=0, bytes_accessed=cost, transcendentals=0),
    )(*front, *ins, *after)


def ready(table):
    def kernel(table, out):
        out[...] = jnp.full(out.shape, table[0], jnp.int32)

    return small_call(kernel, [jax.ShapeDtypeStruct((8, 128), jnp.int32)], (), table)


def join(cap, table, keep, recv, after):
    _, size, blk = keep.shape

    def kernel(table, keep, recv, joined, out):
        joined[...] = keep[...] + recv[...]
        for slot in range(cap):
            out[slot] = joined[table[table_at(cap, 0, SEND) + 1 + slot]]

    return small_call(
        kernel,
        [keep, jax.ShapeDtypeStruct((cap, size, blk), jnp.bfloat16)],
        (keep, recv),
        table,
        after,
    )


def pack(cap, loads, table, joined, after):
    _, size, blk = joined[0].shape
    used = sorted({i for spots in loads for _, i in spots})

    def kernel(table, *refs):
        for spots, out in zip(loads, refs[len(used):]):
            for at, (q, i) in enumerate(spots):
                for slot in range(cap):
                    out[at * cap + slot] = refs[used.index(i)][table[table_at(cap, q, SEND) + 1 + slot]]

    return small_call(
        kernel,
        [jax.ShapeDtypeStruct((len(spots) * cap, size, blk), jnp.bfloat16) for spots in loads],
        [joined[i] for i in used],
        table,
        after,
    )


def has_far(line):
    z, _ = split(lax.axis_index("sector"), Y)
    return (z > 0) & (z < line - 1)


def gather(cap, q, pieces, n_s, table, joined, crossed, after, dtype=jnp.bfloat16, cost=1000, far_in=None, line=0):
    _, size, blk = joined[0].shape
    count = len(pieces)
    spots = [crossed[q, i] for i in pieces]

    def kernel(table, *refs):
        out, total = refs[-2:]
        for k in range(count):
            a, c = refs[k], refs[count + k]
            total[...] = jnp.zeros_like(total)
            at = table_at(cap, q, OWN) + 1
            for slot in range(cap):
                j = table[at + slot]
                total[table[at + cap + slot]] += a[j].astype(jnp.float32)
            at = table_at(cap, q, CROSS) + 1
            for slot in range(cap):
                total[table[at + cap + slot]] += c[spots[k][1] + slot].astype(jnp.float32)
            sums = total[:n_s]
            if far_in is not None:
                sums += jnp.where(has_far(line), refs[2 * count][...].astype(jnp.float32), 0.0)
            out[k * n_s:(k + 1) * n_s] = sums.astype(dtype)

    (out,) = small_call(
        kernel,
        [jax.ShapeDtypeStruct((count * n_s, size, blk), dtype)],
        [joined[i] for i in pieces] + [x for x, _ in spots] + ([] if far_in is None else [far_in]),
        table,
        after,
        [pltpu.VMEM((n_s + 1, size, blk), jnp.float32)],
        cost,
    )
    return out


def advance(cap, n_s, line, step, i, table, joined, crossed, acc, near_in, far_in, after):
    size, blk = joined.shape[1:]
    block = jax.ShapeDtypeStruct((n_s, size, blk), jnp.bfloat16)
    sends = [(step - 1, far_in)] + ([(line - 1 - step, near_in)] if step > 1 else [])
    fresh = sorted({q for q, _ in sends if q not in acc})
    ins, at = [joined], {}
    for q in fresh:
        at[q] = len(ins)
        ins.append(crossed[q, i][0])
    for q, arrived in sends:
        if q not in fresh:
            at[q] = len(ins)
            ins.append(acc[q])
    came = []
    for _, arrived in sends:
        came.append(len(ins))
        if arrived is not None:
            ins.append(arrived)
    saved = [q for q in fresh if step < max(q + 1, line - 1 - q) and step > 1]

    def kernel(*refs):
        if fresh:
            table, refs = refs[0], refs[1:]
        totals = refs[len(refs) - len(fresh):]
        outs = refs[len(ins):]
        for total, q in zip(totals, fresh):
            total[...] = jnp.zeros_like(total)
            spot = table_at(cap, q, OWN) + 1
            for slot in range(cap):
                total[table[spot + cap + slot]] += refs[0][table[spot + slot]].astype(jnp.float32)
            spot = table_at(cap, q, CROSS) + 1
            for slot in range(cap):
                total[table[spot + cap + slot]] += refs[at[q]][crossed[q, i][1] + slot].astype(jnp.float32)
        for k, (q, arrived) in enumerate(sends):
            message = totals[fresh.index(q)][:n_s] if q in fresh else refs[at[q]][...].astype(jnp.float32)
            if arrived is not None:
                extra = refs[came[k]][...].astype(jnp.float32)
                message += jnp.where(has_far(line), extra, 0.0) if k == 0 else extra
            outs[k][...] = message.astype(jnp.bfloat16)
        for k, q in enumerate(saved):
            outs[len(sends) + k][...] = totals[fresh.index(q)][:n_s].astype(jnp.bfloat16)

    outs = small_call(
        kernel,
        [block] * (len(sends) + len(saved)),
        ins,
        table if fresh else None,
        after,
        [pltpu.VMEM((n_s + 1, size, blk), jnp.float32)] * len(fresh),
    )
    for q, x in zip(saved, outs[len(sends):]):
        acc[q] = x
    if step == 1:
        acc[0] = outs[0]
    return outs[:len(sends)]


def finish(n_s, line, piece, rows, base, arrived, out=None):
    size, blk = base.shape[1:]
    half = blk // 2

    def kernel(rows, base, *refs):
        parts, (out, held, sem) = refs[:len(arrived)], refs[-3:]
        row = lax.broadcasted_iota(jnp.int32, (size, blk), 0) + (lax.axis_index("mpo") * half + piece * size)
        inner = has_far(line)
        for p in range(n_s):
            total = base[p] + parts[0][p].astype(jnp.float32)
            for part in parts[1:]:
                total += jnp.where(inner, part[p].astype(jnp.float32), 0.0)
            held[p] = jnp.where(row < rows[p:p + 1], total, 0.0).astype(jnp.bfloat16)
        leave = pltpu.make_async_copy(held, out.at[:, piece * size:(piece + 1) * size], sem)
        leave.start()
        leave.wait()

    ins = [rows, base, *arrived]
    return pl.pallas_call(
        kernel,
        out_shape=jax.ShapeDtypeStruct((n_s, half, blk), jnp.bfloat16),
        in_specs=[VMEM] * len(ins) + ([HBM] if out is not None else []),
        out_specs=HBM,
        scratch_shapes=[pltpu.VMEM((n_s, size, blk), jnp.bfloat16), pltpu.SemaphoreType.DMA],
        input_output_aliases={len(ins): 0} if out is not None else {},
        compiler_params=pltpu.CompilerParams(vmem_limit_bytes=8 * 2**20),
        cost_estimate=pl.CostEstimate(flops=0, bytes_accessed=1000, transcendentals=0),
    )(*ins, *([out] if out is not None else []))


def body(psi, left_env, right_env, term_class, active, dest, sector_rows):
    n = lax.axis_size("sector")
    line = n // Y
    classes, n_s = dest.shape
    cap = (classes * n_s + n - 1) // n + 1
    pieces = [0, 1]
    across = [(d, d ^ 1) for d in range(n)]
    near = [(z * Y + y, (z ^ 1) * Y + y) for z in range(line) for y in range(Y)]
    far = []
    for z in range(line):
        inner = 0 < z < line - 1
        for d in range(z * Y, (z + 1) * Y):
            other = ((((z + 1) ^ 1) - 1) * Y + d % Y) if inner else d
            far += [(d * 2 + core, other * 2 + (core if inner else 1 - core)) for core in range(2)]

    send, keep = shift_sums(psi, left_env, right_env, term_class, active, sector_rows, classes, len(pieces))
    recv = [lax.ppermute(x, "mpo", [(0, 1), (1, 0)]) for x in send]
    table = make_table(n, cap, dest)

    loads = [[(q, i)] for q in range(line - 1) for i in pieces]
    loads.append([(line - 1, i) for i in pieces])
    crossed, joined, came = {}, [], []
    last = ready(table)
    packed = []
    for i in pieces:
        whole, first = join(cap, table, keep[i], recv[i], last)
        joined.append(whole)
        packed.append(first)
        last = [first]
    came = [lax.ppermute(x, "sector", across) for x in packed]
    firsts = pack(cap, loads[2:4], table, joined, last)
    came += [lax.ppermute(x, "sector", across) for x in firsts]
    came += [lax.ppermute(x, "sector", across) for x in pack(cap, loads[4:], table, joined, [firsts[0], came[1]])]
    for spots, x in zip(loads, came):
        for at, spot in enumerate(spots):
            crossed[spot] = (x, at * cap)

    acc = [{} for _ in pieces]
    near_in, far_in = [None for _ in pieces], [None for _ in pieces]
    last = [firsts[0]]
    for step in range(1, line):
        for i in pieces:
            out = advance(cap, n_s, line, step, i, table, joined[i], crossed, acc[i], near_in[i], far_in[i], last)
            last = [out[0]]
            near_in[i] = lax.ppermute(out[0], "sector", near)
            far_in[i] = lax.ppermute(out[1], ("sector", "mpo"), far) if step > 1 else None
    limits = jnp.broadcast_to(sector_rows[:, None], (n_s, psi.shape[2]))
    out = None
    for i in pieces:
        early = far_in[i] if i == 0 else None
        base = gather(
            cap, line - 1, [i], n_s, table, joined, crossed, (), jnp.float32, far_in=early, line=line
        )
        arrived = [near_in[i]] + ([far_in[i]] if i > 0 and far_in[i] is not None else [])
        out = finish(n_s, line, i, limits, base, arrived, out)
    return out


def solution(mesh):
    placed = (
        P(("groups", "sector"), None, None),
        P(("groups", "mpo"), "sector", None, None),
        P(("groups", "mpo"), "sector", None, None),
        P(("groups", "mpo")),
        P(("groups", "mpo"), "sector"),
        P("groups", "sector"),
        P(("groups", "sector")),
    )
    return jax.shard_map(
        body,
        mesh=mesh,
        in_specs=placed,
        out_specs=P(("groups", "sector"), "mpo", None),
        check_vma=False,
    )
```
